32 devices in a mesh: ctx: 16 (over z, x, core), head: 2 (over y).
Axes of the slice: x: 2, y: 2, z: 4, core: 2. Of those that a mesh axis runs over, the one named last changes fastest.
Arguments:
- queries: bfloat16 [16, 256, 32, 128], P('ctx', 'head'), may hold values from -6 to 6
- keys: bfloat16 [16, 256, 4, 128], P('ctx', 'head'), may hold values from -6 to 6
- values: bfloat16 [16, 256, 4, 128], P('ctx', 'head'), may hold values from -6 to 6
Outputs:
- weighted: float32 [16, 256, 32, 128], P('ctx', None, 'head')
- row_max: float32 [32, 16, 256], P('head', 'ctx')
- row_sum: float32 [32, 16, 256], P('head', 'ctx')
The draws below stay inside these ranges and needn't reach their ends.
All inputs are finite; a program needn't handle non-finite values.
Results may differ from the reference program's by a relative error of at most 0.0027.
Values may be sent and summed in bfloat16 or wider, within the bound.
No kernel may reach another device: no remote copies, remote signals or barrier semaphores. Data moves between devices by JAX's collectives and lax.ppermute only.
A program may use at most 64 MiB of HBM per device.

```python
import math
import jax
import jax.numpy as jnp
from jax import lax

HEAD_WIDTH = 128
QUERY_HEADS = 32
KEY_VALUE_HEADS = 4
WIN = 8
SUBBLOCK_TOKENS = 128
PAIRS = 16
SEQUENCE_TOKENS = 4096


def paired_draw(key):
    key_query = jax.random.fold_in(key, 11)
    key_random_seed = jax.random.fold_in(key, 12)
    query_entries = jax.random.truncated_normal(key_query, -6.0, 6.0, (SEQUENCE_TOKENS, QUERY_HEADS, HEAD_WIDTH), jnp.float32)
    key_entries = jax.random.truncated_normal(key_random_seed, -6.0, 6.0, (SEQUENCE_TOKENS, KEY_VALUE_HEADS, HEAD_WIDTH), jnp.float32)
    query_entries = query_entries.reshape(PAIRS, 2 * SUBBLOCK_TOKENS, QUERY_HEADS, HEAD_WIDTH)
    key_entries = key_entries.reshape(PAIRS, 2 * SUBBLOCK_TOKENS, KEY_VALUE_HEADS, HEAD_WIDTH)
    return (query_entries, key_entries)


def draw_queries(key, part):
    return paired_draw(key)[0].astype(jnp.bfloat16)


def draw_keys(key, part):
    return paired_draw(key)[1].astype(jnp.bfloat16)


def level_of(stream_key, dims, cuts, least, largest):
    def one(axis_at, blocks):
        heights = jax.random.uniform(jax.random.fold_in(jax.random.fold_in(stream_key, 6), axis_at), (blocks,), jnp.float32, least / len(cuts), largest / len(cuts))
        return jnp.repeat(jnp.exp(heights), dims[axis_at] // blocks).reshape((-1,) + (1,) * (len(dims) - axis_at - 1))

    level = one(*cuts[0])
    for cut in cuts[1:]:
        level = level * one(*cut)
    return level


def gaussian(stream_key, shape, scale, most, shards=(), kind=jnp.bfloat16):
    level = level_of(stream_key, shape, shards, -0.22, 0.18) if shards else 1.0
    array = jax.random.normal(stream_key, shape, jnp.float32) * scale * level
    return jnp.minimum(jnp.maximum(array, -most), most).astype(kind)


def setup_inputs(seed: int = 0) -> dict:
    seeds = jax.random.split(jax.random.key(seed), 4)
    queries = draw_queries(jax.random.fold_in(seeds[3], 71), 0)
    keys = draw_keys(jax.random.fold_in(seeds[3], 71), 0)
    values = gaussian(seeds[2], (PAIRS, 2 * SUBBLOCK_TOKENS, KEY_VALUE_HEADS, HEAD_WIDTH), 1.0, 6.0, ((0, 16), (1, 2)))
    return {"queries": queries, "keys": keys, "values": values}


def reference(queries, keys, values):
    period_length = PAIRS
    row_halves = SUBBLOCK_TOKENS
    query_group_count = QUERY_HEADS // KEY_VALUE_HEADS
    score_scale = 1.0 / math.sqrt(HEAD_WIDTH)
    row_ids = jnp.arange(row_halves, dtype=jnp.int32)

    def positions(pair_id):
        subs = jnp.stack([2 * pair_id, 2 * period_length - 1 - 2 * pair_id]).astype(jnp.int32)
        return (subs[:, None] * row_halves + row_ids[None, :]).reshape(-1)

    def one_pair(pair_id):
        query_rows = lax.dynamic_index_in_dim(queries, pair_id, 0, keepdims=False).astype(jnp.float32)
        pos_q = positions(pair_id)
        sources = ((pair_id - jnp.arange(WIN, dtype=jnp.int32)) % period_length).astype(jnp.int32)
        pos_k = jax.vmap(positions)(sources).reshape(-1)
        key_row_block = jnp.take(keys, sources, axis=0).reshape(-1, KEY_VALUE_HEADS, HEAD_WIDTH).astype(jnp.float32)
        value_row_block = jnp.take(values, sources, axis=0).reshape(-1, KEY_VALUE_HEADS, HEAD_WIDTH).astype(jnp.float32)
        key_row_block = jnp.repeat(key_row_block, query_group_count, axis=1)
        value_row_block = jnp.repeat(value_row_block, query_group_count, axis=1)
        scores = jnp.einsum('qhd,khd->hqk', query_rows, key_row_block) * score_scale
        visible = pos_k[None, None, :] <= pos_q[None, :, None]
        scores = jnp.where(visible, scores, jnp.float32(-1e+30))
        top_score = lax.optimization_barrier(jnp.max(scores, axis=2))
        weights = jnp.where(visible, jnp.exp(scores - top_score[:, :, None]), jnp.float32(0.0))
        total_weight = lax.optimization_barrier(jnp.sum(weights, axis=2))
        low_weights = weights.astype(jnp.bfloat16).astype(jnp.float32)
        combined = jnp.einsum('hqk,khd->qhd', low_weights, value_row_block)
        return (combined, top_score, total_weight)
    combined, top_score, total_weight = lax.map(one_pair, jnp.arange(period_length, dtype=jnp.int32))
    return (combined, jnp.transpose(top_score, (1, 0, 2)), jnp.transpose(total_weight, (1, 0, 2)))
```

```python
import functools
import math

import jax
import jax.numpy as jnp
from jax import lax
from jax.experimental import pallas as pl
from jax.experimental.pallas import tpu as pltpu
from jax.sharding import PartitionSpec as P

QUERY_HEADS = 32
KEY_VALUE_HEADS = 4
WIN = 8
LAYER = 4
GROUP = QUERY_HEADS // KEY_VALUE_HEADS
BF16 = jnp.bfloat16
F32 = jnp.float32
VMEM_LIMIT = 56 * 2**20
NEG = -1e30


def pack_kernel(count, *refs):
    q_ref, k_ref, v_ref = refs[:3]
    q_outs, kv_outs = refs[3 : 3 + count], refs[3 + count :]
    rows, kv_heads = k_ref.shape[1:3]
    per = kv_heads // count
    h = lax.axis_index("head")
    k = k_ref[0].astype(F32)
    v = v_ref[0].astype(F32)
    for head in range(kv_heads):
        kh = k[:, head, :].astype(BF16)
        vh = v[:, head, :].astype(BF16)
        slot = lax.rem(head // per - h + count, count)
        for d in range(count):

            @pl.when(slot == d)
            def _():
                kv_outs[d][0, head % per] = kh
                kv_outs[d][1, head % per] = vh

    for head in range(kv_heads):
        slot = lax.rem(head // per - h + count, count)
        qh = q_ref[0, :, head * GROUP : (head + 1) * GROUP, :].astype(F32)
        qh = qh.reshape(rows * GROUP, qh.shape[-1]).astype(BF16)
        for d in range(count):

            @pl.when(slot == d)
            def _():
                q_outs[d][head % per] = qh


def pack(queries, keys, values, count):
    rows, width = keys.shape[1], keys.shape[3]
    per = keys.shape[2] // count
    q_shape = jax.ShapeDtypeStruct((per, rows * GROUP, width), BF16)
    kv_shape = jax.ShapeDtypeStruct((2, per, rows, width), BF16)
    outs = pl.pallas_call(
        functools.partial(pack_kernel, count),
        out_shape=(q_shape,) * count + (kv_shape,) * count,
        in_specs=[pl.BlockSpec(memory_space=pltpu.VMEM)] * 3,
        out_specs=[pl.BlockSpec(memory_space=pltpu.VMEM)] * (2 * count),
        compiler_params=pltpu.CompilerParams(vmem_limit_bytes=VMEM_LIMIT),
    )(queries, keys, values)
    return list(outs[:count]), list(outs[count:])


def attend_kernel(n, count, offsets, step_chunks, block, *refs):
    total = len(offsets) * count
    q_hbm, kv_hbm = refs[:count], refs[count : count + total]
    out_ref, max_ref, sum_ref, qbuf, kbuf, vbuf, mbuf, lbuf, qsem, ksem = refs[count + total :]
    per, rows, width = kv_hbm[0].shape[1:]
    half = count * rows // 2
    m_rows = rows * GROUP
    span = step_chunks * rows
    p = lax.axis_index("ctx")
    h = lax.axis_index("head")
    factor = math.log2(math.e) / math.sqrt(width)

    def start_of(pair, chunk):
        r = chunk * rows
        return jnp.where(r < half, 2 * pair * half + r, (2 * n - 2 - 2 * pair) * half + r)

    for s in range(count):
        pltpu.make_async_copy(q_hbm[s], qbuf.at[s], qsem.at[s]).start()
    chunks = []
    for a, offset in enumerate(offsets):
        pair = lax.rem(p - offset(p) + n, n)
        for d in range(count):
            chunks.append(start_of(pair, lax.rem(h - d + count, count)))
    plans = []
    for s in range(count):
        start_q = start_of(p, lax.rem(h - s + count, count))
        seen = jnp.int32(1)
        plan = []
        for c in [s] + [c for c in range(total) if c != s]:
            visible = None if c == s else chunks[c] < start_q
            at = jnp.int32(0) if c == s else seen
            if c != s:
                seen = seen + visible.astype(jnp.int32)
            plan.append((c, visible, at))
        plans.append((plan, seen))

    def copies(s, c, at):
        to = pl.ds(pl.multiple_of(at * rows, rows), rows)
        return (
            pltpu.make_async_copy(kv_hbm[c].at[0], kbuf.at[s, :, to, :], ksem.at[s, c, 0]),
            pltpu.make_async_copy(kv_hbm[c].at[1], vbuf.at[s, :, to, :], ksem.at[s, c, 1]),
        )

    def each(s, act):
        for c, visible, at in plans[s][0]:
            if visible is None:
                act(copies(s, c, at))
            else:

                @pl.when(visible)
                def _():
                    act(copies(s, c, at))

    for s in range(count):
        vbuf[s, :, :span, :] = jnp.zeros((per, span, width), BF16)
    for s in range(count):
        each(s, lambda pair: [x.start() for x in pair])

    for s in range(count):
        q_chunk = lax.rem(h - s + count, count)
        seen = plans[s][1]
        first = lax.rem(seen - 1, step_chunks) + 1
        steps = (seen - first) // step_chunks
        row0 = pl.multiple_of(q_chunk * rows, rows)
        pltpu.make_async_copy(q_hbm[s], qbuf.at[s], qsem.at[s]).wait()
        each(s, lambda pair: [x.wait() for x in pair])
        for g in range(per):

            def out_at(b):
                return (
                    0,
                    pl.ds(row0 + b * (block // GROUP), block // GROUP),
                    slice(g * GROUP, (g + 1) * GROUP),
                    slice(None),
                )

            k = kbuf[s, g, 0:span, :]
            v = vbuf[s, g, 0:span, :]
            for b in range(m_rows // block):
                at = slice(b * block, (b + 1) * block)
                score = lax.dot_general(
                    qbuf[s, g, at, :], k, (((1,), (1,)), ((), ())), preferred_element_type=F32
                )
                col = lax.broadcasted_iota(jnp.int32, (block, span), 1)
                row = (lax.broadcasted_iota(jnp.int32, (block, span), 0) + b * block) // GROUP
                limit = jnp.where(col < rows, row, first * rows - 1)
                score = jnp.where(col <= limit, score, NEG)
                top = jnp.max(score, axis=1, keepdims=True)
                prob = jnp.exp2((score - top) * factor)
                mbuf[at, :] = jnp.broadcast_to(top, (block, 128))
                lbuf[at, :] = sum(prob[:, t : t + 128] for t in range(0, span, 128))
                got = jnp.dot(prob.astype(BF16), v, preferred_element_type=F32)
                out_ref[out_at(b)] = got.reshape(block // GROUP, GROUP, width)

            def step(t, _):
                where = pl.ds(pl.multiple_of((first + t * step_chunks) * rows, rows), span)
                k = kbuf[s, g, where, :]
                v = vbuf[s, g, where, :]
                for b in range(m_rows // block):
                    at = slice(b * block, (b + 1) * block)
                    score = lax.dot_general(
                        qbuf[s, g, at, :], k, (((1,), (1,)), ((), ())), preferred_element_type=F32
                    )
                    old = mbuf[at, :]
                    top = jnp.maximum(old, jnp.max(score, axis=1, keepdims=True))
                    shrink = jnp.exp2((old - top) * factor)
                    probs = [
                        jnp.exp2((score[:, t : t + 128] - top) * factor)
                        for t in range(0, span, 128)
                    ]
                    mbuf[at, :] = top
                    lbuf[at, :] = lbuf[at, :] * shrink + sum(probs)
                    prob = jnp.concatenate([x.astype(BF16) for x in probs], axis=1)
                    got = jnp.dot(prob, v, preferred_element_type=F32)
                    held = out_ref[out_at(b)].reshape(block, width)
                    out_ref[out_at(b)] = (held * shrink + got).reshape(
                        block // GROUP, GROUP, width
                    )
                return 0

            lax.fori_loop(0, steps, step, 0)

            def to_lanes(x):
                x = x.reshape(rows, GROUP, 128)[:, :, :rows]
                a = lax.broadcasted_iota(jnp.int32, (rows, GROUP, rows), 0)
                b = lax.broadcasted_iota(jnp.int32, (rows, GROUP, rows), 2)
                return jnp.sum(jnp.where(a == b, x, 0.0), axis=0)

            tops = to_lanes(mbuf[...]) * (1.0 / math.sqrt(width))
            sums = jnp.sum(lbuf[...], axis=1, keepdims=True)
            sums = to_lanes(jnp.broadcast_to(sums, (m_rows, 128)))
            for d in range(count):

                @pl.when(q_chunk == d)
                def _():
                    max_ref[g * GROUP : (g + 1) * GROUP, 0, d * rows : (d + 1) * rows] = tops
                    sum_ref[g * GROUP : (g + 1) * GROUP, 0, d * rows : (d + 1) * rows] = sums


def attend(q_list, kv_list, offsets, n):
    count = len(q_list)
    per, m_rows, width = q_list[0].shape
    rows = m_rows // GROUP
    step_chunks = 512 // rows
    longest = (len(kv_list) + step_chunks) * rows
    total = len(kv_list)
    return pl.pallas_call(
        functools.partial(attend_kernel, n, count, offsets, step_chunks, min(512, m_rows)),
        out_shape=(
            jax.ShapeDtypeStruct((1, count * rows, per * GROUP, width), F32),
            jax.ShapeDtypeStruct((per * GROUP, 1, count * rows), F32),
            jax.ShapeDtypeStruct((per * GROUP, 1, count * rows), F32),
        ),
        in_specs=[pl.BlockSpec(memory_space=pl.ANY)] * (count + total),
        out_specs=[pl.BlockSpec(memory_space=pltpu.VMEM)] * 3,
        scratch_shapes=[
            pltpu.VMEM((count, per, m_rows, width), BF16),
            pltpu.VMEM((count, per, longest, width), BF16),
            pltpu.VMEM((count, per, longest, width), BF16),
            pltpu.VMEM((m_rows, 128), F32),
            pltpu.VMEM((m_rows, 128), F32),
            pltpu.SemaphoreType.DMA((count,)),
            pltpu.SemaphoreType.DMA((count, total, 2)),
        ],
        compiler_params=pltpu.CompilerParams(vmem_limit_bytes=VMEM_LIMIT),
    )(*q_list, *kv_list)


def along(block, axis, target):
    size = lax.axis_size(axis)
    return lax.ppermute(block, axis, [(i, target(i) % size) for i in range(size)])


def local(queries, keys, values):
    n = lax.axis_size("ctx")
    count = lax.axis_size("head")
    q_out, kv_out = pack(queries, keys, values, count)
    swap = lambda x, d: along(x, "head", lambda i: i + d)
    own = [kv_out[0]] + [swap(kv_out[d], d) for d in range(1, count)]
    q_in = [q_out[0]] + [swap(q_out[d], d) for d in range(1, count)]

    layer = LAYER
    ctx = lambda xs, target: [along(x, "ctx", target) for x in xs]
    up = ctx(own, lambda i: i + layer)
    wide = ctx(own, lambda i: i + 2 if i & 2 == 0 else i + layer + 2)
    near = ctx(own, lambda i: i + 1 if i & 1 == 0 else i + 2 * layer - 1)
    up_x = ctx(up, lambda i: i ^ 2)
    up_c = ctx(up, lambda i: i ^ 1)
    up_xc = ctx(up_x, lambda i: i ^ 1)
    wide_c = ctx(wide, lambda i: i ^ 1)

    def flip(p, bit):
        return jnp.where(lax.rem(p // bit, 2) == 1, bit, -bit)

    wide_at = lambda p: jnp.where(lax.rem(p // 2, 2) == 1, 2, layer + 2)
    near_at = lambda p: jnp.where(lax.rem(p, 2) == 1, 1, 2 * layer - 1)
    offsets = [
        lambda p: 0,
        lambda p: layer,
        wide_at,
        near_at,
        lambda p: layer + flip(p, 2),
        lambda p: layer + flip(p, 1),
        lambda p: layer + flip(p, 1) + flip(p, 2),
        lambda p: flip(p, 1) + wide_at(p),
    ]
    blocks = own + up + wide + near + up_x + up_c + up_xc + wide_c
    return attend(q_in, blocks, offsets, n)


def solution(mesh):
    in_specs = (
        P("ctx", "head", None, None),
        P("ctx", "head", None, None),
        P("ctx", "head", None, None),
    )
    out_specs = (P("ctx", None, "head", None), P("head", "ctx", None), P("head", "ctx", None))
    return jax.shard_map(local, mesh=mesh, in_specs=in_specs, out_specs=out_specs, check_vma=False)
```

```python
import functools
import math

import jax
import jax.numpy as jnp
from jax import lax
from jax.experimental import pallas as pl
from jax.experimental.pallas import tpu as pltpu
from jax.sharding import PartitionSpec as P

QUERY_HEADS = 32
KEY_VALUE_HEADS = 4
WIN = 8
LAYER = 4
GROUP = QUERY_HEADS // KEY_VALUE_HEADS
BF16 = jnp.bfloat16
F32 = jnp.float32
VMEM_LIMIT = 56 * 2**20
NEG = -1e30


def slot_of(head, per, count):
    return lax.rem(head // per - lax.axis_index("head") + count, count)


def pack_kv_kernel(k_ref, v_ref, *outs):
    count = len(outs)
    per = k_ref.shape[2] // count
    k = k_ref[0].astype(F32)
    v = v_ref[0].astype(F32)
    for head in range(k_ref.shape[2]):
        kh = k[:, head, :].astype(BF16)
        vh = v[:, head, :].astype(BF16)
        for d in range(count):

            @pl.when(slot_of(head, per, count) == d)
            def _():
                outs[d][0, head % per] = kh
                outs[d][1, head % per] = vh


def pack_q_kernel(q_ref, *outs):
    count = len(outs)
    rows, heads, width = q_ref.shape[1:]
    per = heads // GROUP // count
    for head in range(heads // GROUP):
        qh = q_ref[0, :, head * GROUP : (head + 1) * GROUP, :].astype(F32)
        qh = qh.reshape(rows * GROUP, width).astype(BF16)
        for d in range(count):

            @pl.when(slot_of(head, per, count) == d)
            def _():
                outs[d][head % per] = qh


def pack(kernel, shape, count, *arrays):
    return pl.pallas_call(
        kernel,
        out_shape=(jax.ShapeDtypeStruct(shape, BF16),) * count,
        in_specs=[pl.BlockSpec(memory_space=pltpu.VMEM)] * len(arrays),
        out_specs=[pl.BlockSpec(memory_space=pltpu.VMEM)] * count,
        compiler_params=pltpu.CompilerParams(vmem_limit_bytes=VMEM_LIMIT),
    )(*arrays)


def attend_kernel(n, count, singles, offsets, step_chunks, block, *refs):
    total = len(offsets) * count
    merged = len(offsets) - singles // count
    q_hbm, refs = refs[:count], refs[count:]
    kv_hbm, refs = list(refs[:singles]), refs[singles:]
    kv_hbm += [refs[a].at[d] for a in range(merged) for d in range(count)]
    out_ref, max_ref, sum_ref, qbuf, kbuf, vbuf, mbuf, lbuf, qsem, ksem = refs[merged:]
    per, rows, width = kv_hbm[0].shape[1:]
    half = count * rows // 2
    m_rows = rows * GROUP
    span = step_chunks * rows
    p = lax.axis_index("ctx")
    h = lax.axis_index("head")
    factor = math.log2(math.e) / math.sqrt(width)

    def start_of(pair, chunk):
        r = chunk * rows
        return jnp.where(r < half, 2 * pair * half + r, (2 * n - 2 - 2 * pair) * half + r)

    for s in range(count):
        pltpu.make_async_copy(q_hbm[s], qbuf.at[s], qsem.at[s]).start()
    chunks = []
    for a, offset in enumerate(offsets):
        pair = lax.rem(p - offset(p) + n, n)
        for d in range(count):
            chunks.append(start_of(pair, lax.rem(h - d + count, count)))
    plans = []
    for s in range(count):
        start_q = start_of(p, lax.rem(h - s + count, count))
        seen = jnp.int32(1)
        plan = []
        for c in [s] + [c for c in range(total) if c != s]:
            visible = None if c == s else chunks[c] < start_q
            at = jnp.int32(0) if c == s else seen
            if c != s:
                seen = seen + visible.astype(jnp.int32)
            plan.append((c, visible, at))
        plans.append((plan, seen))

    def copies(s, c, at):
        to = pl.ds(pl.multiple_of(at * rows, rows), rows)
        return (
            pltpu.make_async_copy(kv_hbm[c].at[0], kbuf.at[s, :, to, :], ksem.at[s, c, 0]),
            pltpu.make_async_copy(kv_hbm[c].at[1], vbuf.at[s, :, to, :], ksem.at[s, c, 1]),
        )

    def each(s, act):
        for c, visible, at in plans[s][0]:
            if visible is None:
                act(copies(s, c, at))
            else:

                @pl.when(visible)
                def _():
                    act(copies(s, c, at))

    for s in range(count):
        vbuf[s, :, :span, :] = jnp.zeros((per, span, width), BF16)
    for s in range(count):
        each(s, lambda pair: [x.start() for x in pair])

    for s in range(count):
        q_chunk = lax.rem(h - s + count, count)
        seen = plans[s][1]
        first = lax.rem(seen - 1, step_chunks) + 1
        steps = (seen - first) // step_chunks
        row0 = pl.multiple_of(q_chunk * rows, rows)
        pltpu.make_async_copy(q_hbm[s], qbuf.at[s], qsem.at[s]).wait()
        each(s, lambda pair: [x.wait() for x in pair])
        for g in range(per):

            def out_at(b):
                return (
                    0,
                    pl.ds(row0 + b * (block // GROUP), block // GROUP),
                    slice(g * GROUP, (g + 1) * GROUP),
                    slice(None),
                )

            k = kbuf[s, g, 0:span, :]
            v = vbuf[s, g, 0:span, :]
            for b in range(m_rows // block):
                at = slice(b * block, (b + 1) * block)
                score = lax.dot_general(
                    qbuf[s, g, at, :], k, (((1,), (1,)), ((), ())), preferred_element_type=F32
                )
                col = lax.broadcasted_iota(jnp.int32, (block, span), 1)
                row = (lax.broadcasted_iota(jnp.int32, (block, span), 0) + b * block) // GROUP
                limit = jnp.where(col < rows, row, first * rows - 1)
                score = jnp.where(col <= limit, score, NEG)
                top = jnp.max(score, axis=1, keepdims=True)
                prob = jnp.exp2((score - top) * factor)
                mbuf[at, :] = jnp.broadcast_to(top, (block, 128))
                lbuf[at, :] = sum(prob[:, t : t + 128] for t in range(0, span, 128))
                got = jnp.dot(prob.astype(BF16), v, preferred_element_type=F32)
                out_ref[out_at(b)] = got.reshape(block // GROUP, GROUP, width)

            def step(t, _):
                where = pl.ds(pl.multiple_of((first + t * step_chunks) * rows, rows), span)
                k = kbuf[s, g, where, :]
                v = vbuf[s, g, where, :]
                for b in range(m_rows // block):
                    at = slice(b * block, (b + 1) * block)
                    score = lax.dot_general(
                        qbuf[s, g, at, :], k, (((1,), (1,)), ((), ())), preferred_element_type=F32
                    )
                    old = mbuf[at, :]
                    top = jnp.maximum(old, jnp.max(score, axis=1, keepdims=True))
                    shrink = jnp.exp2((old - top) * factor)
                    probs = [
                        jnp.exp2((score[:, t : t + 128] - top) * factor)
                        for t in range(0, span, 128)
                    ]
                    mbuf[at, :] = top
                    lbuf[at, :] = lbuf[at, :] * shrink + sum(probs)
                    prob = jnp.concatenate([x.astype(BF16) for x in probs], axis=1)
                    got = jnp.dot(prob, v, preferred_element_type=F32)
                    held = out_ref[out_at(b)].reshape(block, width)
                    out_ref[out_at(b)] = (held * shrink + got).reshape(
                        block // GROUP, GROUP, width
                    )
                return 0

            lax.fori_loop(0, steps, step, 0)

            def to_lanes(x):
                x = x.reshape(rows, GROUP, 128)[:, :, :rows]
                a = lax.broadcasted_iota(jnp.int32, (rows, GROUP, rows), 0)
                b = lax.broadcasted_iota(jnp.int32, (rows, GROUP, rows), 2)
                return jnp.sum(jnp.where(a == b, x, 0.0), axis=0)

            tops = to_lanes(mbuf[...]) * (1.0 / math.sqrt(width))
            sums = jnp.sum(lbuf[...], axis=1, keepdims=True)
            sums = to_lanes(jnp.broadcast_to(sums, (m_rows, 128)))
            for d in range(count):

                @pl.when(q_chunk == d)
                def _():
                    max_ref[g * GROUP : (g + 1) * GROUP, 0, d * rows : (d + 1) * rows] = tops
                    sum_ref[g * GROUP : (g + 1) * GROUP, 0, d * rows : (d + 1) * rows] = sums


def attend(q_list, kv_list, merged, offsets, n):
    count = len(q_list)
    per, m_rows, width = q_list[0].shape
    rows = m_rows // GROUP
    step_chunks = 512 // rows
    total = len(offsets) * count
    longest = (total + step_chunks) * rows
    return pl.pallas_call(
        functools.partial(attend_kernel, n, count, len(kv_list), offsets, step_chunks, min(512, m_rows)),
        out_shape=(
            jax.ShapeDtypeStruct((1, count * rows, per * GROUP, width), F32),
            jax.ShapeDtypeStruct((per * GROUP, 1, count * rows), F32),
            jax.ShapeDtypeStruct((per * GROUP, 1, count * rows), F32),
        ),
        in_specs=[pl.BlockSpec(memory_space=pl.ANY)] * (count + len(kv_list) + len(merged)),
        out_specs=[pl.BlockSpec(memory_space=pltpu.VMEM)] * 3,
        scratch_shapes=[
            pltpu.VMEM((count, per, m_rows, width), BF16),
            pltpu.VMEM((count, per, longest, width), BF16),
            pltpu.VMEM((count, per, longest, width), BF16),
            pltpu.VMEM((m_rows, 128), F32),
            pltpu.VMEM((m_rows, 128), F32),
            pltpu.SemaphoreType.DMA((count,)),
            pltpu.SemaphoreType.DMA((count, total, 2)),
        ],
        compiler_params=pltpu.CompilerParams(vmem_limit_bytes=VMEM_LIMIT),
    )(*q_list, *kv_list, *merged)


def along(block, axis, target):
    size = lax.axis_size(axis)
    return lax.ppermute(block, axis, [(i, target(i) % size) for i in range(size)])


def local(queries, keys, values):
    n = lax.axis_size("ctx")
    count = lax.axis_size("head")
    rows, kv_heads, width = keys.shape[1:]
    per = kv_heads // count
    me = lax.axis_index("ctx")
    swap = lambda x, d: along(x, "head", lambda i: i + d)
    ctx = lambda xs, target: [along(x, "ctx", target) for x in xs]

    kv = pack(pack_kv_kernel, (2, per, rows, width), count, keys, values)
    own = [kv[0]] + [swap(kv[d], d) for d in range(1, count)]
    q = pack(pack_q_kernel, (per, rows * GROUP, width), count, queries)
    q = [q[0]] + [swap(q[d], d) for d in range(1, count)]

    layer = LAYER
    up = ctx(own, lambda i: i + layer)
    far = ctx(up, lambda i: i + layer // 2)
    odd = ctx(up, lambda i: i + layer - 1 if i & 1 else i + 1)
    column = lax.rem(me // 2, 2) == 0
    side = jnp.concatenate([jnp.where(column, a, b)[None] for a, b in zip(own, up)])
    side = along(side, "ctx", lambda i: i ^ 2)
    core = lax.rem(me, 2) == 0
    next_to = jnp.concatenate([jnp.where(core, a, b)[None] for a, b in zip(own, up)])
    next_to = along(next_to, "ctx", lambda i: i ^ 1)
    far_c = ctx(far, lambda i: i ^ 1)
    side_c = along(side, "ctx", lambda i: i ^ 1)

    bit = lambda p, even, other: jnp.where(lax.rem(p, 2) == 0, even, other)
    offsets = [
        lambda p: 0,
        lambda p: layer,
        lambda p: layer + 2,
        lambda p: bit(p, layer + 3, layer + 1),
        lambda p: bit(p, layer + 1, layer + 3),
        lambda p: 2,
        lambda p: bit(p, 3, 1),
        lambda p: bit(p, 1, 3),
    ]
    blocks = own + up + far + odd + far_c
    return attend(q, blocks, [side, next_to, side_c], offsets, n)


def solution(mesh):
    in_specs = (
        P("ctx", "head", None, None),
        P("ctx", "head", None, None),
        P("ctx", "head", None, None),
    )
    out_specs = (P("ctx", None, "head", None), P("head", "ctx", None), P("head", "ctx", None))
    return jax.shard_map(local, mesh=mesh, in_specs=in_specs, out_specs=out_specs, check_vma=False)
```

```python
import functools
import math

import jax
import jax.numpy as jnp
from jax import lax
from jax.experimental import pallas as pl
from jax.experimental.pallas import tpu as pltpu
from jax.sharding import PartitionSpec as P

QUERY_HEADS = 32
KEY_VALUE_HEADS = 4
WIN = 8
LAYER = 4
GROUP = QUERY_HEADS // KEY_VALUE_HEADS
BF16 = jnp.bfloat16
F32 = jnp.float32
VMEM_LIMIT = 56 * 2**20
NEG = -1e30
SPAN = 512
BLOCK = 128
AHEAD = 0


def slot_of(head, per, count):
    return lax.rem(head // per - lax.axis_index("head") + count, count)


def pack_kv_kernel(k_ref, v_ref, *outs):
    count = len(outs)
    per = k_ref.shape[2] // count
    k = k_ref[0].astype(F32)
    v = v_ref[0].astype(F32)
    for head in range(k_ref.shape[2]):
        kh = k[:, head, :].astype(BF16)
        vh = v[:, head, :].astype(BF16)
        for d in range(count):

            @pl.when(slot_of(head, per, count) == d)
            def _():
                outs[d][0, head % per] = kh
                outs[d][1, head % per] = vh


def pack_q_kernel(q_ref, *outs):
    count = len(outs)
    rows, heads, width = q_ref.shape[1:]
    per = heads // GROUP // count
    for head in range(heads // GROUP):
        qh = q_ref[0, :, head * GROUP : (head + 1) * GROUP, :].astype(F32)
        qh = qh.reshape(rows * GROUP, width).astype(BF16)
        for d in range(count):

            @pl.when(slot_of(head, per, count) == d)
            def _():
                outs[d][head % per] = qh


def pack(kernel, shape, count, *arrays):
    return pl.pallas_call(
        kernel,
        out_shape=(jax.ShapeDtypeStruct(shape, BF16),) * count,
        in_specs=[pl.BlockSpec(memory_space=pltpu.VMEM)] * len(arrays),
        out_specs=[pl.BlockSpec(memory_space=pltpu.VMEM)] * count,
        compiler_params=pltpu.CompilerParams(vmem_limit_bytes=VMEM_LIMIT),
    )(*arrays)


def attend_kernel(n, count, singles, offsets, step_chunks, block, *refs):
    total = len(offsets) * count
    merged = len(offsets) - singles // count
    q_hbm, refs = refs[:count], refs[count:]
    kv_hbm, refs = refs[: singles + merged], refs[singles + merged :]
    out_hbm, max_ref, sum_ref, qbuf, kvbuf, acc, mbuf, lbuf, order, qsem, ksem, osem = refs
    per, m_rows, width = q_hbm[0].shape
    rows = m_rows // GROUP
    half = count * rows // 2
    span = step_chunks * rows
    p = lax.axis_index("ctx")
    h = lax.axis_index("head")
    factor = math.log2(math.e) / math.sqrt(width)

    loads = [pltpu.make_async_copy(q_hbm[s], qbuf.at[s], qsem.at[s]) for s in range(count)]
    for i, ref in enumerate(kv_hbm):
        if i < singles:
            to = kvbuf.at[i]
        else:
            to = kvbuf.at[pl.ds(singles + (i - singles) * count, count)]
        loads.append(pltpu.make_async_copy(ref, to, ksem.at[i]))
    for load in loads:
        load.start()

    def start_of(pair, chunk):
        r = chunk * rows
        return jnp.where(r < half, 2 * pair * half + r, (2 * n - 2 - 2 * pair) * half + r)

    chunk_of = [lax.rem(h - d + count, count) for d in range(count)]
    starts = []
    for offset in offsets:
        pair = lax.rem(p - offset(p) + n, n)
        starts += [start_of(pair, chunk) for chunk in chunk_of]
    firsts, steps = [], []
    for s in range(count):
        for t in range(step_chunks):
            order[s, t] = s
        seen = jnp.int32(1)
        for c in range(total):
            if c != s:
                visible = (starts[c] < starts[s]).astype(jnp.int32)
                order[s, seen] = lax.select(visible == 1, c, s)
                seen = seen + visible
        first = lax.rem(seen - 1, step_chunks) + 1
        firsts.append(first)
        steps.append((seen - first) // step_chunks)

    def keys_at(s, g, begin):
        at = [order[s, begin + t] for t in range(step_chunks)]
        return jnp.concatenate([kvbuf[i, 0, g] for i in at], axis=0)

    def values_at(s, g, begin):
        at = [order[s, begin + t] for t in range(step_chunks)]
        v = jnp.concatenate([kvbuf[i, 1, g] for i in at], axis=0)
        return jnp.concatenate([v, jnp.ones((span, 128), BF16)], axis=1)

    def score_of(s, g, b, k):
        q = qbuf[s, g, b * block : (b + 1) * block, :]
        return lax.dot_general(q, k, (((1,), (1,)), ((), ())), preferred_element_type=F32)

    def acc_at(s, g, b):
        row = b * (block // GROUP)
        return s, slice(row, row + block // GROUP), slice(g * GROUP, (g + 1) * GROUP)

    def tiles(x):
        return [x[:, t : t + 128] for t in range(0, span, 128)]

    def first_block(s, g, b, score, v):
        at = slice(b * block, (b + 1) * block)
        shape = (block // GROUP, GROUP, 128)
        row = lax.broadcasted_iota(jnp.int32, shape, 0) + b * (block // GROUP)
        col = lax.broadcasted_iota(jnp.int32, shape, 2)
        parts = []
        for t, x in enumerate(tiles(score)):
            x = x.reshape(shape)
            if t * 128 >= rows and rows % 128 == 0:
                x = jnp.where(t * 128 < firsts[s] * rows, x, NEG)
            else:
                seen = col + t * 128 < firsts[s] * rows
                if t * 128 < rows:
                    seen &= (col + t * 128 <= row) | (col + t * 128 >= rows)
                x = jnp.where(seen, x, NEG)
            parts.append(x.reshape(block, 128))
        top = jnp.max(functools.reduce(jnp.maximum, parts), axis=1, keepdims=True)
        prob = jnp.concatenate(
            [jnp.exp2((x - top) * factor).astype(BF16) for x in parts], axis=1
        )
        got = jnp.dot(prob, v, preferred_element_type=F32)
        mbuf[s, g, at, :] = jnp.broadcast_to(top, (block, 128))
        lbuf[s, g, at, :] = got[:, width:]
        acc[acc_at(s, g, b)] = got[:, :width].reshape(block // GROUP, GROUP, width)

    def next_block(s, g, b, score, v):
        at = slice(b * block, (b + 1) * block)
        parts = tiles(score)
        old = mbuf[s, g, at, :]
        top = jnp.maximum(
            old, jnp.max(functools.reduce(jnp.maximum, parts), axis=1, keepdims=True)
        )
        shrink = jnp.exp2((old - top) * factor)
        prob = jnp.concatenate(
            [jnp.exp2((x - top) * factor).astype(BF16) for x in parts], axis=1
        )
        got = jnp.dot(prob, v, preferred_element_type=F32)
        mbuf[s, g, at, :] = top
        lbuf[s, g, at, :] = lbuf[s, g, at, :] * shrink + got[:, width:]
        held = acc[acc_at(s, g, b)].reshape(block, width)
        acc[acc_at(s, g, b)] = (held * shrink + got[:, :width]).reshape(
            block // GROUP, GROUP, width
        )

    def run(work, begin, finish):
        scores, keys, vals = {}, {}, {}
        for i in range(len(work) + AHEAD):
            if i < len(work):
                s, g, b = work[i]
                if (s, g) not in keys:
                    keys[s, g] = keys_at(s, g, begin)
                scores[i] = score_of(s, g, b, keys[s, g])
            if i >= AHEAD:
                s, g, b = work[i - AHEAD]
                if (s, g) not in vals:
                    vals[s, g] = values_at(s, g, begin)
                finish(s, g, b, scores.pop(i - AHEAD), vals[s, g])

    def to_lanes(x):
        x = x.reshape(rows, GROUP, 128)[:, :, :rows]
        a = lax.broadcasted_iota(jnp.int32, (rows, GROUP, rows), 0)
        b = lax.broadcasted_iota(jnp.int32, (rows, GROUP, rows), 2)
        return jnp.sum(jnp.where(a == b, x, 0.0), axis=0)

    for load in loads:
        load.wait()
    blocks = [(g, b) for g in range(per) for b in range(m_rows // block)]
    run([(s, g, b) for s in range(count) for g, b in blocks], 0, first_block)
    saves = []
    for s in range(count):

        def step(t, _):
            run([(s, g, b) for g, b in blocks], firsts[s] + t * step_chunks, next_block)
            return 0

        lax.fori_loop(0, steps[s], step, 0)
        row0 = pl.multiple_of(chunk_of[s] * rows, rows)
        saves.append(
            pltpu.make_async_copy(acc.at[s], out_hbm.at[0, pl.ds(row0, rows)], osem.at[s])
        )
        saves[-1].start()
        for g in range(per):
            tops = to_lanes(mbuf[s, g]) * (1.0 / math.sqrt(width))
            sums = to_lanes(lbuf[s, g])
            for d in range(count):

                @pl.when(chunk_of[s] == d)
                def _():
                    max_ref[g * GROUP : (g + 1) * GROUP, 0, d * rows : (d + 1) * rows] = tops
                    sum_ref[g * GROUP : (g + 1) * GROUP, 0, d * rows : (d + 1) * rows] = sums
    for save in saves:
        save.wait()


def attend(q_list, kv_list, merged, offsets, n):
    count = len(q_list)
    per, m_rows, width = q_list[0].shape
    rows = m_rows // GROUP
    total = len(offsets) * count
    step_chunks = SPAN // rows
    loads = len(kv_list) + len(merged)
    return pl.pallas_call(
        functools.partial(
            attend_kernel, n, count, len(kv_list), offsets, step_chunks, min(BLOCK, m_rows)
        ),
        out_shape=(
            jax.ShapeDtypeStruct((1, count * rows, per * GROUP, width), F32),
            jax.ShapeDtypeStruct((per * GROUP, 1, count * rows), F32),
            jax.ShapeDtypeStruct((per * GROUP, 1, count * rows), F32),
        ),
        in_specs=[pl.BlockSpec(memory_space=pl.ANY)] * (count + loads),
        out_specs=[pl.BlockSpec(memory_space=pl.ANY)]
        + [pl.BlockSpec(memory_space=pltpu.VMEM)] * 2,
        scratch_shapes=[
            pltpu.VMEM((count, per, m_rows, width), BF16),
            pltpu.VMEM((total, 2, per, rows, width), BF16),
            pltpu.VMEM((count, rows, per * GROUP, width), F32),
            pltpu.VMEM((count, per, m_rows, 128), F32),
            pltpu.VMEM((count, per, m_rows, 128), F32),
            pltpu.SMEM((count, total + 1 + step_chunks), jnp.int32),
            pltpu.SemaphoreType.DMA((count,)),
            pltpu.SemaphoreType.DMA((loads,)),
            pltpu.SemaphoreType.DMA((count,)),
        ],
        compiler_params=pltpu.CompilerParams(vmem_limit_bytes=VMEM_LIMIT),
    )(*q_list, *kv_list, *merged)


def along(block, axis, target):
    size = lax.axis_size(axis)
    return lax.ppermute(block, axis, [(i, target(i) % size) for i in range(size)])


def local(queries, keys, values):
    n = lax.axis_size("ctx")
    count = lax.axis_size("head")
    rows, kv_heads, width = keys.shape[1:]
    per = kv_heads // count
    me = lax.axis_index("ctx")
    swap = lambda x, d: along(x, "head", lambda i: i + d)
    ctx = lambda xs, target: [along(x, "ctx", target) for x in xs]

    kv = pack(pack_kv_kernel, (2, per, rows, width), count, keys, values)
    own = [kv[0]] + [swap(kv[d], d) for d in range(1, count)]
    q = pack(pack_q_kernel, (per, rows * GROUP, width), count, queries)
    q = [q[0]] + [swap(q[d], d) for d in range(1, count)]

    layer = LAYER
    up = ctx(own, lambda i: i + layer)
    far = ctx(up, lambda i: i + layer // 2)
    odd = ctx(up, lambda i: i + layer - 1 if i & 1 else i + 1)
    column = lax.rem(me // 2, 2) == 0
    side = jnp.concatenate([jnp.where(column, a, b)[None] for a, b in zip(own, up)])
    side = along(side, "ctx", lambda i: i ^ 2)
    core = lax.rem(me, 2) == 0
    next_to = jnp.concatenate([jnp.where(core, a, b)[None] for a, b in zip(own, up)])
    next_to = along(next_to, "ctx", lambda i: i ^ 1)
    far_c = ctx(far, lambda i: i ^ 1)
    side_c = along(side, "ctx", lambda i: i ^ 1)

    bit = lambda p, even, other: jnp.where(lax.rem(p, 2) == 0, even, other)
    offsets = [
        lambda p: 0,
        lambda p: layer,
        lambda p: layer + 2,
        lambda p: bit(p, layer + 3, layer + 1),
        lambda p: bit(p, layer + 1, layer + 3),
        lambda p: 2,
        lambda p: bit(p, 3, 1),
        lambda p: bit(p, 1, 3),
    ]
    blocks = own + up + far + odd + far_c
    return attend(q, blocks, [side, next_to, side_c], offsets, n)


def solution(mesh):
    in_specs = (
        P("ctx", "head", None, None),
        P("ctx", "head", None, None),
        P("ctx", "head", None, None),
    )
    out_specs = (P("ctx", None, "head", None), P("head", "ctx", None), P("head", "ctx", None))
    return jax.shard_map(local, mesh=mesh, in_specs=in_specs, out_specs=out_specs, check_vma=False)
```

```python
import functools
import math

import jax
import jax.numpy as jnp
from jax import lax
from jax.experimental import pallas as pl
from jax.experimental.pallas import tpu as pltpu
from jax.sharding import PartitionSpec as P

QUERY_HEADS = 32
KEY_VALUE_HEADS = 4
WIN = 8
LAYER = 4
GROUP = QUERY_HEADS // KEY_VALUE_HEADS
BF16 = jnp.bfloat16
F32 = jnp.float32
VMEM_LIMIT = 20 * 2**20
NEG = -1e30
SPAN = 512
BLOCK = 128
COST = 10**9
PACK_LIMIT = 56 * 2**20


def slot_of(head, per, count):
    return lax.rem(head // per - lax.axis_index("head") + count, count)


def place(outs, head, per, at, x):
    for d in range(len(outs)):

        @pl.when(slot_of(head, per, len(outs)) == d)
        def _():
            outs[d][at + (head % per,)] = x


def pack_kv_kernel(k_hbm, v_hbm, *refs):
    outs, (flat, wide, sems) = refs[:-3], refs[-3:]
    rows, heads, width = k_hbm.shape[1:]
    loads = [
        pltpu.make_async_copy(ref.at[0], flat.at[i], sems.at[i])
        for i, ref in enumerate((k_hbm, v_hbm))
    ]
    for load in loads:
        load.start()
    for i in range(2):
        loads[i].wait()
        wide.at[i].reshape(rows, 8, width)[:, :heads, :] = flat[i].astype(F32)
        for head in range(heads):
            x = wide[i, pl.ds(head, rows, stride=8), :].astype(BF16)
            place(outs, head, heads // len(outs), (i,), x)


def pack_kv(keys, values, count):
    rows, heads, width = keys.shape[1:]
    shape = jax.ShapeDtypeStruct((2, heads // count, rows, width), BF16)
    return pl.pallas_call(
        pack_kv_kernel,
        out_shape=(shape,) * count,
        in_specs=[pl.BlockSpec(memory_space=pl.ANY)] * 2,
        out_specs=[pl.BlockSpec(memory_space=pltpu.VMEM)] * count,
        scratch_shapes=[
            pltpu.VMEM((2, rows, heads, width), BF16),
            pltpu.VMEM((2, rows * 8, width), F32),
            pltpu.SemaphoreType.DMA((2,)),
        ],
        compiler_params=pltpu.CompilerParams(vmem_limit_bytes=PACK_LIMIT),
    )(keys, values)


def pack_q_kernel(q_ref, *outs):
    rows, heads, width = q_ref.shape[1:]
    for head in range(heads // GROUP):
        x = q_ref[0, :, head * GROUP : (head + 1) * GROUP, :].astype(F32)
        x = x.reshape(rows * GROUP, width).astype(BF16)
        place(outs, head, heads // GROUP // len(outs), (), x)


def pack_q(queries, count):
    rows, heads, width = queries.shape[1:]
    shape = jax.ShapeDtypeStruct((heads // GROUP // count, rows * GROUP, width), BF16)
    return pl.pallas_call(
        pack_q_kernel,
        out_shape=(shape,) * count,
        in_specs=[pl.BlockSpec(memory_space=pltpu.VMEM)],
        out_specs=[pl.BlockSpec(memory_space=pltpu.VMEM)] * count,
        compiler_params=pltpu.CompilerParams(vmem_limit_bytes=VMEM_LIMIT),
    )(queries)


def attend_kernel(n, count, slots, singles, offsets, block, begin, end, *refs):
    total = len(offsets) * count
    here = len(slots)
    loads_n = singles + (total - singles) // count
    q_hbm, refs = refs[:here], refs[here:]
    kv_hbm, refs = refs[:loads_n], refs[loads_n:]
    if not begin:
        refs = refs[3 * here :]
    if end:
        out_hbm, max_ref, sum_ref = refs[:3]
        refs = refs[3:]
    acc, mbuf, lbuf = refs[:here], refs[here : 2 * here], refs[2 * here : 3 * here]
    qbuf, kvbuf, order, qsem, ksem, osem = refs[3 * here :]
    per, m_rows, width = q_hbm[0].shape
    rows = m_rows // GROUP
    half = count * rows // 2
    small, large = SPAN // 2 // rows, SPAN // rows
    p = lax.axis_index("ctx")
    h = lax.axis_index("head")
    factor = math.log2(math.e) / math.sqrt(width)

    loads = [pltpu.make_async_copy(q_hbm[s], qbuf.at[s], qsem.at[s]) for s in range(here)]
    for i, ref in enumerate(kv_hbm):
        if i < singles:
            to = kvbuf.at[i]
        else:
            to = kvbuf.at[pl.ds(singles + (i - singles) * count, count)]
        loads.append(pltpu.make_async_copy(ref, to, ksem.at[i]))
    for load in loads:
        load.start()

    def start_of(pair, chunk):
        r = chunk * rows
        return jnp.where(r < half, 2 * pair * half + r, (2 * n - 2 - 2 * pair) * half + r)

    chunk_of = [lax.rem(h - d + count, count) for d in range(count)]
    starts = []
    for offset in offsets:
        pair = lax.rem(p - offset(p) + n, n)
        starts += [start_of(pair, chunk) for chunk in chunk_of]
    seen = []
    for s, slot in enumerate(slots):
        mine = start_of(p, chunk_of[slot])
        found = jnp.int32(0)
        if begin:
            order[s, 0] = slot
            found = jnp.int32(1)
        for c in range(total):
            if not begin or c != slot:
                order[s, found] = c
                found = found + (starts[c] < mine).astype(jnp.int32)
        for t in range(large):
            order[s, found + t] = 0
        seen.append(found)

    def chunks_at(kind, s, g, at, chunks):
        return jnp.concatenate(
            [kvbuf[order[s, at + t], kind, g] for t in range(chunks)], axis=0
        )

    def tiles(x):
        return [x[:, t : t + 128] for t in range(0, x.shape[1], 128)]

    def one(s, g, b, k, v, at, diagonal, partial):
        where = slice(b * block, (b + 1) * block)
        row = b * (block // GROUP)
        acc_at = slice(row, row + block // GROUP), slice(g * GROUP, (g + 1) * GROUP)
        score = lax.dot_general(
            qbuf[s, g, where, :], k, (((1,), (1,)), ((), ())), preferred_element_type=F32
        )
        parts = tiles(score)
        if diagonal or partial:
            shape = (block // GROUP, GROUP, 128)
            col = lax.broadcasted_iota(jnp.int32, shape, 2)
            row = lax.broadcasted_iota(jnp.int32, shape, 0) + row
            left = (seen[s] - at) * rows
            for t, x in enumerate(parts):
                x = x.reshape(shape)
                if rows % 128 == 0 and (t * 128 >= rows or not diagonal):
                    if t or diagonal:
                        x = jnp.where(t * 128 < left, x, NEG)
                else:
                    ok = col + t * 128 < left
                    if diagonal and t * 128 < rows:
                        ok &= (col + t * 128 <= row) | (col + t * 128 >= rows)
                    x = jnp.where(ok, x, NEG)
                parts[t] = x.reshape(block, 128)
        top = jnp.max(functools.reduce(jnp.maximum, parts), axis=1, keepdims=True)
        if not diagonal:
            old = mbuf[s][g, where, :]
            top = jnp.maximum(old, top)
        prob = jnp.concatenate(
            [jnp.exp2((x - top) * factor).astype(BF16) for x in parts], axis=1
        )
        got = jnp.dot(prob, v, preferred_element_type=F32)
        gain, mass = got[:, :width], got[:, width:]
        if not diagonal:
            shrink = jnp.exp2((old - top) * factor)
            gain = acc[s][acc_at].reshape(block, width) * shrink + gain
            mass = lbuf[s][g, where, :] * shrink + mass
        mbuf[s][g, where, :] = jnp.broadcast_to(top, (block, 128))
        lbuf[s][g, where, :] = mass
        acc[s][acc_at] = gain.reshape(block // GROUP, GROUP, width)

    def run(s, at, chunks, diagonal=False, partial=False):
        for g in range(per):
            k = chunks_at(0, s, g, at, chunks)
            v = chunks_at(1, s, g, at, chunks)
            v = jnp.concatenate([v, jnp.ones((chunks * rows, 128), BF16)], axis=1)
            for b in range(m_rows // block):
                one(s, g, b, k, v, at, diagonal, partial)

    def to_lanes(x):
        x = x.reshape(rows, GROUP, 128)[:, :, :rows]
        a = lax.broadcasted_iota(jnp.int32, (rows, GROUP, rows), 0)
        b = lax.broadcasted_iota(jnp.int32, (rows, GROUP, rows), 2)
        return jnp.sum(jnp.where(a == b, x, 0.0), axis=0)

    for load in loads:
        load.wait()
    base = small if begin else 0
    if begin:
        for s in range(here):
            run(s, 0, small, diagonal=True)
    saves = []
    for s, slot in enumerate(slots):
        left = jnp.maximum(seen[s] - base, 0)
        full = left // large
        rest = (left - full * large + small - 1) // small

        def whole(t, _):
            run(s, base + t * large, large)
            return 0

        def part(t, _):
            run(s, base + full * large + t * small, small, partial=True)
            return 0

        lax.fori_loop(0, full, whole, 0)
        lax.fori_loop(0, rest, part, 0)
        if not end:
            continue
        row0 = pl.multiple_of(chunk_of[slot] * rows, rows)
        saves.append(
            pltpu.make_async_copy(acc[s], out_hbm.at[0, pl.ds(row0, rows)], osem.at[s])
        )
        saves[-1].start()
        for g in range(per):
            tops = to_lanes(mbuf[s][g]) * (1.0 / math.sqrt(width))
            sums = to_lanes(lbuf[s][g])
            for d in range(count):

                @pl.when(chunk_of[slot] == d)
                def _():
                    max_ref[g * GROUP : (g + 1) * GROUP, 0, d * rows : (d + 1) * rows] = tops
                    sum_ref[g * GROUP : (g + 1) * GROUP, 0, d * rows : (d + 1) * rows] = sums
    for save in saves:
        save.wait()


def attend(q_list, slots, kv_list, merged, offsets, n, state, end):
    count, here = len(q_list), len(slots)
    per, m_rows, width = q_list[0].shape
    rows = m_rows // GROUP
    total = len(offsets) * count
    loads = len(kv_list) + len(merged)
    begin = state is None
    near, away = pl.BlockSpec(memory_space=pltpu.VMEM), pl.BlockSpec(memory_space=pl.ANY)
    held = [jax.ShapeDtypeStruct((rows, per * GROUP, width), F32)] * here
    held += [jax.ShapeDtypeStruct((per, m_rows, 128), F32)] * (2 * here)
    out_shape, out_specs, aliases = [], [], {}
    if end:
        out_shape += [
            jax.ShapeDtypeStruct((1, count * rows, per * GROUP, width), F32),
            jax.ShapeDtypeStruct((per * GROUP, 1, count * rows), F32),
            jax.ShapeDtypeStruct((per * GROUP, 1, count * rows), F32),
        ]
        out_specs += [away, near, near]
    if not begin:
        aliases = {here + loads + i: len(out_shape) + i for i in range(3 * here)}
    out_shape += held
    out_specs += [near] * len(held)
    outs = pl.pallas_call(
        functools.partial(
            attend_kernel, n, count, slots, len(kv_list), offsets, min(BLOCK, m_rows), begin, end
        ),
        out_shape=out_shape,
        in_specs=[away] * (here + loads) + [near] * (0 if begin else len(held)),
        out_specs=out_specs,
        input_output_aliases=aliases,
        scratch_shapes=[
            pltpu.VMEM((here, per, m_rows, width), BF16),
            pltpu.VMEM((total, 2, per, rows, width), BF16),
            pltpu.SMEM((here, total + 1 + SPAN // rows), jnp.int32),
            pltpu.SemaphoreType.DMA((here,)),
            pltpu.SemaphoreType.DMA((loads,)),
            pltpu.SemaphoreType.DMA((here,)),
        ],
        compiler_params=pltpu.CompilerParams(vmem_limit_bytes=VMEM_LIMIT),
        cost_estimate=pl.CostEstimate(
            flops=COST * len(offsets) * here, bytes_accessed=2**20, transcendentals=0
        ),
    )(*[q_list[s] for s in slots], *kv_list, *merged, *(state or []))
    if end:
        return tuple(outs[:3])
    return [outs[i * here : (i + 1) * here] for i in range(3)]


def join(*states):
    return [x for part in zip(*states) for xs in part for x in xs]


def along(block, axis, target):
    size = lax.axis_size(axis)
    return lax.ppermute(block, axis, [(i, target(i) % size) for i in range(size)])


def climb(block, d, layer):
    n, count = lax.axis_size("ctx"), lax.axis_size("head")
    edges = []
    for p in range(n):
        for h in range(count):
            edges.append((p * count + h, (p + layer) % n * count + (h + d) % count))
    return lax.ppermute(block, ("ctx", "head"), edges)


def local(queries, keys, values):
    n = lax.axis_size("ctx")
    count = lax.axis_size("head")
    me = lax.axis_index("ctx")
    swap = lambda x, d: along(x, "head", lambda i: i + d)

    kv = pack_kv(keys, values, count)
    q = pack_q(queries, count)
    own = [kv[0]] + [swap(kv[d], d) for d in range(1, count)]

    layer = LAYER
    up = jnp.stack([climb(x, d, layer) for d, x in enumerate(kv)])
    q = [q[0]] + [swap(q[d], d) for d in range(1, count)]

    both = lax.optimization_barrier(jnp.stack(own))
    side = along(both, "ctx", lambda i: i + layer // 2)
    far = along(up, "ctx", lambda i: i + layer // 2)
    odd = along(up, "ctx", lambda i: i + layer - 1 if i & 1 else i + 1)
    near = jnp.where(lax.rem(me, 2) == 0, both, up)
    near = along(near, "ctx", lambda i: i ^ 1)
    side_c = along(side, "ctx", lambda i: i ^ 1)

    bit = lambda p, even, other: jnp.where(lax.rem(p, 2) == 0, even, other)
    offsets = [
        lambda p: 0,
        lambda p: layer,
        lambda p: layer + 2,
        lambda p: bit(p, layer + 3, layer + 1),
        lambda p: bit(p, layer + 1, layer + 3),
        lambda p: 2,
        lambda p: bit(p, 3, 1),
        lambda p: bit(p, 1, 3),
    ]
    own_at, up_at, far_at, odd_at, far_c_at, side_at, near_at, side_c_at = offsets
    slots = list(range(count))
    early = [both, up, near], [own_at, up_at, near_at], n
    state = join(attend(q, slots, [], *early, None, False))
    state, far = lax.optimization_barrier((state, far))
    far_c = along(far, "ctx", lambda i: i ^ 1)
    late = [side, side_c, odd, far, far_c], [side_at, side_c_at, odd_at, far_at, far_c_at], n
    return attend(q, slots, [], *late, state, True)


def solution(mesh):
    in_specs = (
        P("ctx", "head", None, None),
        P("ctx", "head", None, None),
        P("ctx", "head", None, None),
    )
    out_specs = (P("ctx", None, "head", None), P("head", "ctx", None), P("head", "ctx", None))
    return jax.shard_map(local, mesh=mesh, in_specs=in_specs, out_specs=out_specs, check_vma=False)
```

```python
import functools
import math

import jax
import jax.numpy as jnp
from jax import lax
from jax.experimental import pallas as pl
from jax.experimental.pallas import tpu as pltpu
from jax.sharding import PartitionSpec as P

QUERY_HEADS = 32
KEY_VALUE_HEADS = 4
WIN = 8
LAYER = 4
GROUP = QUERY_HEADS // KEY_VALUE_HEADS
BF16 = jnp.bfloat16
F32 = jnp.float32
VMEM_LIMIT = 20 * 2**20
NEG = -1e30
SPAN = 256
BLOCK = 128
COST = 10**9
PACK_LIMIT = 56 * 2**20


def slot_of(head, per, count):
    return lax.rem(head // per - lax.axis_index("head") + count, count)


def place(outs, head, per, at, x):
    for d in range(len(outs)):

        @pl.when(slot_of(head, per, len(outs)) == d)
        def _():
            outs[d][at + (head % per,)] = x


def pack_kv_kernel(k_hbm, v_hbm, *refs):
    outs, (flat, wide, sems) = refs[:-3], refs[-3:]
    rows, heads, width = k_hbm.shape[1:]
    loads = [
        pltpu.make_async_copy(ref.at[0], flat.at[i], sems.at[i])
        for i, ref in enumerate((k_hbm, v_hbm))
    ]
    for load in loads:
        load.start()
    for i in range(2):
        loads[i].wait()
        wide.at[i].reshape(rows, 8, width)[:, :heads, :] = flat[i].astype(F32)
        for head in range(heads):
            x = wide[i, pl.ds(head, rows, stride=8), :].astype(BF16)
            place(outs, head, heads // len(outs), (i,), x)


def pack_kv(keys, values, count):
    rows, heads, width = keys.shape[1:]
    shape = jax.ShapeDtypeStruct((2, heads // count, rows, width), BF16)
    return pl.pallas_call(
        pack_kv_kernel,
        out_shape=(shape,) * count,
        in_specs=[pl.BlockSpec(memory_space=pl.ANY)] * 2,
        out_specs=[pl.BlockSpec(memory_space=pltpu.VMEM)] * count,
        scratch_shapes=[
            pltpu.VMEM((2, rows, heads, width), BF16),
            pltpu.VMEM((2, rows * 8, width), F32),
            pltpu.SemaphoreType.DMA((2,)),
        ],
        compiler_params=pltpu.CompilerParams(vmem_limit_bytes=PACK_LIMIT),
    )(keys, values)


def pack_q_kernel(count, q_ref, own, *away):
    rows, heads, width = q_ref.shape[1:]
    per = heads // GROUP // count
    split = len(away) // max(count - 1, 1)
    for head in range(heads // GROUP):
        x = q_ref[0, :, head * GROUP : (head + 1) * GROUP, :].astype(F32)
        x = x.reshape(rows * GROUP, width).astype(BF16)
        part, g = divmod(head % per, per // split) if away else (0, 0)
        for d in range(count):

            @pl.when(slot_of(head, per, count) == d)
            def _():
                if d:
                    away[(d - 1) * split + part][g] = x
                else:
                    own[head % per] = x


def pack_q(queries, count, split):
    rows, heads, width = queries.shape[1:]
    per = heads // GROUP // count
    own = jax.ShapeDtypeStruct((per, rows * GROUP, width), BF16)
    away = jax.ShapeDtypeStruct((per // split, rows * GROUP, width), BF16)
    outs = (own,) + (away,) * (split * (count - 1))
    return pl.pallas_call(
        functools.partial(pack_q_kernel, count),
        out_shape=outs,
        in_specs=[pl.BlockSpec(memory_space=pltpu.VMEM)],
        out_specs=[pl.BlockSpec(memory_space=pltpu.VMEM)] * len(outs),
        compiler_params=pltpu.CompilerParams(vmem_limit_bytes=VMEM_LIMIT),
    )(queries)


def start_of(pair, chunk, n, count, rows, pick):
    half = count * rows // 2
    r = chunk * rows
    return pick(r < half, 2 * pair * half + r, (2 * n - 2 - 2 * pair) * half + r)


def step_range(n, count, rows, offsets, begin, small):
    pick = lambda c, x, y: x if c else y
    found = []
    for p in range(n):
        steps = 0
        for chunk in range(count):
            mine = start_of(p, chunk, n, count, rows, pick)
            seen = sum(
                start_of((p - offset(p)) % n, c, n, count, rows, pick) < mine
                for offset in offsets
                for c in range(count)
            )
            seen = max(seen + 1 - small, 0) if begin else seen
            steps += -(-seen // small)
        found.append(steps)
    return min(found), max(found)


def attend_kernel(n, count, parts, offsets, block, begin, end, *refs):
    total = len(offsets) * count
    if begin:
        q_hbm, refs = refs[:count], refs[count:]
    kv_hbm, refs = refs[: len(offsets)], refs[len(offsets) :]
    held = 4 * len(parts)
    if not begin:
        refs = refs[held:]
    if end:
        out_hbm, max_ref, sum_ref = refs[:3]
        refs = refs[3:]
    states = [refs[i : i + 4] for i in range(0, held, 4)]
    kvbuf, order, qsem, ksem, osem = refs[held:]
    per, m_rows, width = states[0][0].shape[1:]
    rows = m_rows // GROUP
    small = SPAN // rows
    p = lax.axis_index("ctx")
    h = lax.axis_index("head")
    factor = math.log2(math.e) / math.sqrt(width)

    loads = []
    if begin:
        mine = q_hbm[0].at[pl.ds(parts[0] * per, per)]
        for s, ref in enumerate([mine, *q_hbm[1:]]):
            loads.append(pltpu.make_async_copy(ref, states[0][0].at[s], qsem.at[s]))
    for i, ref in enumerate(kv_hbm):
        to = kvbuf.at[pl.ds(i * count, count)]
        ref = ref.at[:, :, pl.ds(parts[0] * per, len(parts) * per)]
        loads.append(pltpu.make_async_copy(ref, to, ksem.at[i]))
    for load in loads:
        load.start()

    chunk_of = [lax.rem(h - d + count, count) for d in range(count)]
    starts = []
    for offset in offsets:
        pair = lax.rem(p - offset(p) + n, n)
        starts += [start_of(pair, chunk, n, count, rows, jnp.where) for chunk in chunk_of]
    seen, ends = [], [jnp.int32(0)]
    base = small if begin else 0
    for s in range(count):
        mine = start_of(p, chunk_of[s], n, count, rows, jnp.where)
        found = jnp.int32(0)
        if begin:
            order[s, 0] = s
            found = jnp.int32(1)
        for c in range(total):
            if not begin or c != s:
                order[s, found] = c
                found = found + (starts[c] < mine).astype(jnp.int32)
        again = order[s, jnp.maximum(found - 1, 0)]
        for t in range(small):
            order[s, found + t] = again
        seen.append(found)
        ends.append(ends[-1] + (jnp.maximum(found - base, 0) + small - 1) // small)

    def chunks_at(kind, s, g, at):
        return [kvbuf[order[s, at + t], kind, g] for t in range(small)]

    def one(part, s, g, b, k, v, left, diagonal):
        qbuf, acc, mbuf, lbuf = states[part]
        where = slice(b * block, (b + 1) * block)
        row = b * (block // GROUP)
        acc_at = s, slice(row, row + block // GROUP), slice(g * GROUP, (g + 1) * GROUP)
        score = lax.dot_general(
            qbuf[s, g, where, :], k, (((1,), (1,)), ((), ())), preferred_element_type=F32
        )
        parts = [score[:, t : t + 128] for t in range(0, small * rows, 128)]
        if diagonal:
            shape = (block // GROUP, GROUP, 128)
            col = lax.broadcasted_iota(jnp.int32, shape, 2)
            row = lax.broadcasted_iota(jnp.int32, shape, 0) + row
            for t, x in enumerate(parts):
                x = x.reshape(shape)
                if t * 128 >= rows and rows % 128 == 0:
                    x = jnp.where(t * 128 < left, x, NEG)
                else:
                    ok = col + t * 128 < left
                    if t * 128 < rows:
                        ok &= (col + t * 128 <= row) | (col + t * 128 >= rows)
                    x = jnp.where(ok, x, NEG)
                parts[t] = x.reshape(block, 128)
        top = jnp.max(functools.reduce(jnp.maximum, parts), axis=1, keepdims=True)
        if not diagonal:
            old = mbuf[s, g, where, :]
            top = jnp.maximum(old, top)
        prob = jnp.concatenate(
            [jnp.exp2((x - top) * factor).astype(BF16) for x in parts], axis=1
        )
        got = jnp.dot(prob, v, preferred_element_type=F32)
        gain, mass = got[:, :width], got[:, width:]
        if not diagonal:
            shrink = jnp.exp2((old - top) * factor)
            gain = acc[acc_at].reshape(block, width) * shrink + gain
            mass = lbuf[s, g, where, :] * shrink + mass
        mbuf[s, g, where, :] = jnp.broadcast_to(top, (block, 128))
        lbuf[s, g, where, :] = mass
        acc[acc_at] = gain.reshape(block // GROUP, GROUP, width)

    def run(s, at, found, diagonal):
        left = (found - at) * rows
        for g in range(len(parts) * per):
            k = jnp.concatenate(chunks_at(0, s, g, at), axis=0)
            v = [jnp.concatenate([x, jnp.ones_like(x)], axis=1) for x in chunks_at(1, s, g, at)]
            if not diagonal:
                v[1:] = [
                    jnp.where(t * rows < left, x, jnp.zeros_like(x))
                    for t, x in enumerate(v[1:], 1)
                ]
            v = jnp.concatenate(v, axis=0)
            for b in range(m_rows // block):
                one(g // per, s, g % per, b, k, v, left, diagonal)

    def step(t):
        s, at, found = jnp.int32(0), base + t * small, seen[0]
        for c in range(1, count):
            after = t >= ends[c]
            s = jnp.where(after, c, s)
            at = jnp.where(after, base + (t - ends[c]) * small, at)
            found = jnp.where(after, seen[c], found)
        run(s, at, found, False)

    def to_lanes(x):
        x = x.reshape(rows, GROUP, 128)[:, :, :rows]
        a = lax.broadcasted_iota(jnp.int32, (rows, GROUP, rows), 0)
        b = lax.broadcasted_iota(jnp.int32, (rows, GROUP, rows), 2)
        return jnp.sum(jnp.where(a == b, x, 0.0), axis=0)

    for load in loads:
        load.wait()
    if begin:
        for s in range(count):
            run(s, 0, seen[s], True)
    least, most = step_range(n, count, rows, offsets, begin, small)
    for t in range(least):
        step(t)
    for t in range(least, most):

        @pl.when(t < ends[-1])
        def _():
            step(t)

    if not end:
        return
    saves = []
    heads = per * GROUP
    for i, part in enumerate(parts):
        for s in range(count):
            row0 = pl.multiple_of(chunk_of[s] * rows, rows)
            to = out_hbm.at[0, pl.ds(row0, rows), pl.ds(part * heads, heads)]
            saves.append(pltpu.make_async_copy(states[i][1].at[s], to, osem.at[i, s]))
            saves[-1].start()
    for i, part in enumerate(parts):
        _, _, mbuf, lbuf = states[i]
        for s in range(count):
            for g in range(per):
                tops = to_lanes(mbuf[s, g]) * (1.0 / math.sqrt(width))
                sums = to_lanes(lbuf[s, g])
                at = slice(part * heads + g * GROUP, part * heads + (g + 1) * GROUP)
                for d in range(count):

                    @pl.when(chunk_of[s] == d)
                    def _():
                        max_ref[at, 0, d * rows : (d + 1) * rows] = tops
                        sum_ref[at, 0, d * rows : (d + 1) * rows] = sums
    for save in saves:
        save.wait()


def attend(q_list, kv_list, offsets, parts, split, n, state, end):
    begin = state is None
    count, all_heads, rows, width = kv_list[0].shape[0], *kv_list[0].shape[2:]
    per = all_heads // split
    m_rows = rows * GROUP
    near, away = pl.BlockSpec(memory_space=pltpu.VMEM), pl.BlockSpec(memory_space=pl.ANY)
    held = [
        jax.ShapeDtypeStruct((count, per, m_rows, width), BF16),
        jax.ShapeDtypeStruct((count, rows, per * GROUP, width), F32),
        jax.ShapeDtypeStruct((count, per, m_rows, 128), F32),
        jax.ShapeDtypeStruct((count, per, m_rows, 128), F32),
    ] * len(parts)
    out_shape, out_specs, aliases = [], [], {}
    if end:
        out_shape += [
            jax.ShapeDtypeStruct((1, count * rows, all_heads * GROUP, width), F32),
            jax.ShapeDtypeStruct((all_heads * GROUP, 1, count * rows), F32),
            jax.ShapeDtypeStruct((all_heads * GROUP, 1, count * rows), F32),
        ]
        out_specs += [away, near, near]
    given = len(q_list) + len(kv_list)
    if not begin:
        aliases = {given + i: len(out_shape) + i for i in range(len(held))}
    out_shape += held
    out_specs += [near] * len(held)
    total = len(offsets) * count
    outs = pl.pallas_call(
        functools.partial(
            attend_kernel, n, count, parts, offsets, min(BLOCK, m_rows), begin, end
        ),
        out_shape=out_shape,
        in_specs=[away] * given + [near] * (0 if begin else len(held)),
        out_specs=out_specs,
        input_output_aliases=aliases,
        scratch_shapes=[
            pltpu.VMEM((total, 2, len(parts) * per, rows, width), BF16),
            pltpu.SMEM((count, total + 1 + SPAN // rows), jnp.int32),
            pltpu.SemaphoreType.DMA((count,)),
            pltpu.SemaphoreType.DMA((len(offsets),)),
            pltpu.SemaphoreType.DMA((len(parts), count)),
        ],
        compiler_params=pltpu.CompilerParams(vmem_limit_bytes=VMEM_LIMIT),
        cost_estimate=pl.CostEstimate(
            flops=COST * len(offsets) * len(parts), bytes_accessed=2**20, transcendentals=0
        ),
    )(*q_list, *kv_list, *(state or []))
    return tuple(outs[:3]) if end else outs


def along(block, axis, target):
    size = lax.axis_size(axis)
    return lax.ppermute(block, axis, [(i, target(i) % size) for i in range(size)])


def climb(block, d, layer):
    n, count = lax.axis_size("ctx"), lax.axis_size("head")
    edges = []
    for p in range(n):
        for h in range(count):
            edges.append((p * count + h, (p + layer) % n * count + (h + d) % count))
    return lax.ppermute(block, ("ctx", "head"), edges)


def local(queries, keys, values):
    n = lax.axis_size("ctx")
    count = lax.axis_size("head")
    me = lax.axis_index("ctx")
    swap = lambda x, d: along(x, "head", lambda i: i + d)

    kv = pack_kv(keys, values, count)
    own = [kv[0]] + [swap(kv[d], d) for d in range(1, count)]

    layer = LAYER
    up = jnp.stack([climb(x, d, layer) for d, x in enumerate(kv)])
    split = 2 if own[0].shape[1] % 2 == 0 else 1
    q_own, *q_away = pack_q(queries, count, split)
    q = [
        [q_own] + [swap(q_away[(d - 1) * split + part], d) for d in range(1, count)]
        for part in range(split)
    ]

    both = lax.optimization_barrier(jnp.stack(own))
    side = along(both, "ctx", lambda i: i + layer // 2)
    far = along(up, "ctx", lambda i: i + layer // 2)
    odd = along(up, "ctx", lambda i: i + layer - 1 if i & 1 else i + 1)
    near = jnp.where(lax.rem(me, 2) == 0, both, up)
    near = along(near, "ctx", lambda i: i ^ 1)
    side_c = along(side, "ctx", lambda i: i ^ 1)

    bit = lambda p, even, other: even + (other - even) * (p & 1)
    offsets = [
        lambda p: 0,
        lambda p: layer,
        lambda p: layer + 2,
        lambda p: bit(p, layer + 3, layer + 1),
        lambda p: bit(p, layer + 1, layer + 3),
        lambda p: 2,
        lambda p: bit(p, 3, 1),
        lambda p: bit(p, 1, 3),
    ]
    own_at, up_at, far_at, odd_at, far_c_at, side_at, near_at, side_c_at = offsets
    first = [both, up, near, side], [own_at, up_at, near_at, side_at]
    state = [x for i in range(split) for x in attend(q[i], *first, [i], split, n, None, False)]
    state, far = lax.optimization_barrier((state, far))
    far_c = along(far, "ctx", lambda i: i ^ 1)
    parts = list(range(split))
    state = attend([], [side_c, odd, far], [side_c_at, odd_at, far_at], parts, split, n, state, False)
    return attend([], [far_c], [far_c_at], parts, split, n, state, True)


def solution(mesh):
    in_specs = (
        P("ctx", "head", None, None),
        P("ctx", "head", None, None),
        P("ctx", "head", None, None),
    )
    out_specs = (P("ctx", None, "head", None), P("head", "ctx", None), P("head", "ctx", None))
    return jax.shard_map(local, mesh=mesh, in_specs=in_specs, out_specs=out_specs, check_vma=False)
```

```python
import functools
import math

import jax
import jax.numpy as jnp
from jax import lax
from jax.experimental import pallas as pl
from jax.experimental.pallas import tpu as pltpu
from jax.sharding import PartitionSpec as P

QUERY_HEADS = 32
KEY_VALUE_HEADS = 4
WIN = 8
LAYER = 4
GROUP = QUERY_HEADS // KEY_VALUE_HEADS
BF16 = jnp.bfloat16
F32 = jnp.float32
VMEM_LIMIT = 20 * 2**20
NEG = -1e30
SPAN = 256
BLOCK = 128
COST = 10**9
PACK_LIMIT = 56 * 2**20


def slot_of(head, per, count):
    return lax.rem(head // per - lax.axis_index("head") + count, count)


def place(outs, head, per, at, x):
    for d in range(len(outs)):

        @pl.when(slot_of(head, per, len(outs)) == d)
        def _():
            outs[d][at + (head % per,)] = x


def pack_kv_kernel(k_hbm, v_hbm, *refs):
    outs, (flat, wide, sems) = refs[:-3], refs[-3:]
    rows, heads, width = k_hbm.shape[1:]
    loads = [
        pltpu.make_async_copy(ref.at[0], flat.at[i], sems.at[i])
        for i, ref in enumerate((k_hbm, v_hbm))
    ]
    for load in loads:
        load.start()
    for i in range(2):
        loads[i].wait()
        wide.at[i].reshape(rows, 8, width)[:, :heads, :] = flat[i].astype(F32)
        for head in range(heads):
            x = wide[i, pl.ds(head, rows, stride=8), :].astype(BF16)
            place(outs, head, heads // len(outs), (i,), x)


def pack_kv(keys, values, count):
    rows, heads, width = keys.shape[1:]
    shape = jax.ShapeDtypeStruct((2, heads // count, rows, width), BF16)
    return pl.pallas_call(
        pack_kv_kernel,
        out_shape=(shape,) * count,
        in_specs=[pl.BlockSpec(memory_space=pl.ANY)] * 2,
        out_specs=[pl.BlockSpec(memory_space=pltpu.VMEM)] * count,
        scratch_shapes=[
            pltpu.VMEM((2, rows, heads, width), BF16),
            pltpu.VMEM((2, rows * 8, width), F32),
            pltpu.SemaphoreType.DMA((2,)),
        ],
        compiler_params=pltpu.CompilerParams(vmem_limit_bytes=PACK_LIMIT),
    )(keys, values)


def pack_q_kernel(count, q_ref, own, *away):
    rows, heads, width = q_ref.shape[1:]
    per = heads // GROUP // count
    split = len(away) // max(count - 1, 1)
    for head in range(heads // GROUP):
        x = q_ref[0, :, head * GROUP : (head + 1) * GROUP, :].astype(F32)
        x = x.reshape(rows * GROUP, width).astype(BF16)
        part, g = divmod(head % per, per // split) if away else (0, 0)
        for d in range(count):

            @pl.when(slot_of(head, per, count) == d)
            def _():
                if d:
                    away[(d - 1) * split + part][g] = x
                else:
                    own[head % per] = x


def pack_q(queries, count, split):
    rows, heads, width = queries.shape[1:]
    per = heads // GROUP // count
    own = jax.ShapeDtypeStruct((per, rows * GROUP, width), BF16)
    away = jax.ShapeDtypeStruct((per // split, rows * GROUP, width), BF16)
    outs = (own,) + (away,) * (split * (count - 1))
    return pl.pallas_call(
        functools.partial(pack_q_kernel, count),
        out_shape=outs,
        in_specs=[pl.BlockSpec(memory_space=pltpu.VMEM)],
        out_specs=[pl.BlockSpec(memory_space=pltpu.VMEM)] * len(outs),
        compiler_params=pltpu.CompilerParams(vmem_limit_bytes=VMEM_LIMIT),
    )(queries)


def start_of(pair, chunk, n, count, rows, pick):
    half = count * rows // 2
    r = chunk * rows
    return pick(r < half, 2 * pair * half + r, (2 * n - 2 - 2 * pair) * half + r)


def step_range(n, count, rows, offsets, begin, small):
    pick = lambda c, x, y: x if c else y
    found = []
    for p in range(n):
        steps = 0
        for chunk in range(count):
            mine = start_of(p, chunk, n, count, rows, pick)
            seen = sum(
                start_of((p - offset(p)) % n, c, n, count, rows, pick) < mine
                for offset in offsets
                for c in range(count)
            )
            seen = max(seen + 1 - small, 0) if begin else seen
            steps += -(-seen // small)
        found.append(steps)
    return min(found), max(found)


def attend_kernel(n, count, parts, offsets, block, begin, end, *refs):
    total = len(offsets) * count
    if begin:
        q_hbm, refs = refs[:count], refs[count:]
    kv_hbm, refs = refs[: len(offsets)], refs[len(offsets) :]
    held = 4 * len(parts)
    if not begin:
        refs = refs[held:]
    if end:
        out_hbm, max_hbm, sum_hbm = refs[:3]
        refs = refs[3:]
    states = [refs[i : i + 4] for i in range(0, held, 4)]
    kvbuf, tops_buf, sums_buf, order, qsem, ksem, osem = refs[held:]
    per, m_rows, width = states[0][0].shape[1:]
    rows = m_rows // GROUP
    small = SPAN // rows
    p = lax.axis_index("ctx")
    h = lax.axis_index("head")
    factor = math.log2(math.e) / math.sqrt(width)

    loads = []
    if begin:
        mine = q_hbm[0].at[pl.ds(parts[0] * per, per)]
        for s, ref in enumerate([mine, *q_hbm[1:]]):
            loads.append(pltpu.make_async_copy(ref, states[0][0].at[s], qsem.at[s]))
    for i, ref in enumerate(kv_hbm):
        to = kvbuf.at[pl.ds(i * count, count)]
        ref = ref.at[:, :, pl.ds(parts[0] * per, len(parts) * per)]
        loads.append(pltpu.make_async_copy(ref, to, ksem.at[i]))
    for load in loads:
        load.start()

    chunk_of = [lax.rem(h - d + count, count) for d in range(count)]
    starts = []
    for offset in offsets:
        pair = lax.rem(p - offset(p) + n, n)
        starts += [start_of(pair, chunk, n, count, rows, jnp.where) for chunk in chunk_of]
    seen, ends = [], [jnp.int32(0)]
    base = small if begin else 0
    for s in range(count):
        mine = start_of(p, chunk_of[s], n, count, rows, jnp.where)
        found = jnp.int32(0)
        if begin:
            order[s, 0] = s
            found = jnp.int32(1)
        for c in range(total):
            if not begin or c != s:
                order[s, found] = c
                found = found + (starts[c] < mine).astype(jnp.int32)
        again = order[s, jnp.maximum(found - 1, 0)]
        for t in range(small):
            order[s, found + t] = again
        seen.append(found)
        ends.append(ends[-1] + (jnp.maximum(found - base, 0) + small - 1) // small)

    def chunks_at(kind, s, g, at):
        return [kvbuf[order[s, at + t], kind, g] for t in range(small)]

    def one(part, s, g, b, k, v, left, diagonal):
        qbuf, acc, mbuf, lbuf = states[part]
        where = slice(b * block, (b + 1) * block)
        row = b * (block // GROUP)
        acc_at = s, slice(row, row + block // GROUP), slice(g * GROUP, (g + 1) * GROUP)
        score = lax.dot_general(
            qbuf[s, g, where, :], k, (((1,), (1,)), ((), ())), preferred_element_type=F32
        )
        parts = [score[:, t : t + 128] for t in range(0, small * rows, 128)]
        if diagonal:
            shape = (block // GROUP, GROUP, 128)
            col = lax.broadcasted_iota(jnp.int32, shape, 2)
            row = lax.broadcasted_iota(jnp.int32, shape, 0) + row
            for t, x in enumerate(parts):
                x = x.reshape(shape)
                if t * 128 >= rows and rows % 128 == 0:
                    x = jnp.where(t * 128 < left, x, NEG)
                else:
                    ok = col + t * 128 < left
                    if t * 128 < rows:
                        ok &= (col + t * 128 <= row) | (col + t * 128 >= rows)
                    x = jnp.where(ok, x, NEG)
                parts[t] = x.reshape(block, 128)
        top = jnp.max(functools.reduce(jnp.maximum, parts), axis=1, keepdims=True)
        if not diagonal:
            old = mbuf[s, g, where, :]
            top = jnp.maximum(old, top)
        prob = jnp.concatenate(
            [jnp.exp2((x - top) * factor).astype(BF16) for x in parts], axis=1
        )
        got = jnp.dot(prob, v, preferred_element_type=F32)
        gain, mass = got[:, :width], got[:, width:]
        if not diagonal:
            shrink = jnp.exp2((old - top) * factor)
            gain = acc[acc_at].reshape(block, width) * shrink + gain
            mass = lbuf[s, g, where, :] * shrink + mass
        mbuf[s, g, where, :] = jnp.broadcast_to(top, (block, 128))
        lbuf[s, g, where, :] = mass
        acc[acc_at] = gain.reshape(block // GROUP, GROUP, width)

    def run(s, at, found, diagonal):
        left = (found - at) * rows
        for g in range(len(parts) * per):
            k = jnp.concatenate(chunks_at(0, s, g, at), axis=0)
            v = [jnp.concatenate([x, jnp.ones_like(x)], axis=1) for x in chunks_at(1, s, g, at)]
            if not diagonal:
                v[1:] = [
                    jnp.where(t * rows < left, x, jnp.zeros_like(x))
                    for t, x in enumerate(v[1:], 1)
                ]
            v = jnp.concatenate(v, axis=0)
            for b in range(m_rows // block):
                one(g // per, s, g % per, b, k, v, left, diagonal)

    def step(t):
        s, at, found = jnp.int32(0), base + t * small, seen[0]
        for c in range(1, count):
            after = t >= ends[c]
            s = jnp.where(after, c, s)
            at = jnp.where(after, base + (t - ends[c]) * small, at)
            found = jnp.where(after, seen[c], found)
        run(s, at, found, False)

    for load in loads:
        load.wait()
    if begin:
        for s in range(count):
            run(s, 0, seen[s], True)
    least, most = step_range(n, count, rows, offsets, begin, small)
    for t in range(least):
        step(t)
    for t in range(least, most):

        @pl.when(t < ends[-1])
        def _():
            step(t)

    if not end:
        return
    saves = []
    heads = per * GROUP
    for s in range(count):
        row0 = pl.multiple_of(chunk_of[s] * rows, rows)
        for i, part in enumerate(parts):
            to = out_hbm.at[0, pl.ds(row0, rows), pl.ds(part * heads, heads)]
            saves.append(pltpu.make_async_copy(states[i][1].at[s], to, osem.at[i, s]))
            saves[-1].start()

    lane = lax.broadcasted_iota(jnp.int32, (GROUP, 128), 1)
    for s in range(count):
        picked = [jnp.zeros((GROUP, 128), F32)] * (2 * len(parts) * per)
        for r in range(rows):
            at = slice(r * GROUP, (r + 1) * GROUP)
            found = [states[i][j][s, g, at, :] for i in range(len(parts)) for g in range(per) for j in (2, 3)]
            picked = [jnp.where(lane == r, x, old) for x, old in zip(found, picked)]
        tops = jnp.concatenate(picked[0::2], axis=0)[:, :rows] * (1.0 / math.sqrt(width))
        sums = jnp.concatenate(picked[1::2], axis=0)[:, :rows]
        for d in range(count):

            @pl.when(chunk_of[s] == d)
            def _():
                tops_buf[:, 0, d * rows : (d + 1) * rows] = tops
                sums_buf[:, 0, d * rows : (d + 1) * rows] = sums
    saves.append(pltpu.make_async_copy(tops_buf, max_hbm, qsem.at[0]))
    saves.append(pltpu.make_async_copy(sums_buf, sum_hbm, ksem.at[0]))
    for save in saves[-2:]:
        save.start()
    for save in saves:
        save.wait()


def attend(q_list, kv_list, offsets, parts, split, n, state, end):
    begin = state is None
    count, all_heads, rows, width = kv_list[0].shape[0], *kv_list[0].shape[2:]
    per = all_heads // split
    m_rows = rows * GROUP
    near, away = pl.BlockSpec(memory_space=pltpu.VMEM), pl.BlockSpec(memory_space=pl.ANY)
    held = [
        jax.ShapeDtypeStruct((count, per, m_rows, width), BF16),
        jax.ShapeDtypeStruct((count, rows, per * GROUP, width), F32),
        jax.ShapeDtypeStruct((count, per, m_rows, 128), F32),
        jax.ShapeDtypeStruct((count, per, m_rows, 128), F32),
    ] * len(parts)
    out_shape, out_specs, aliases = [], [], {}
    if end:
        out_shape += [
            jax.ShapeDtypeStruct((1, count * rows, all_heads * GROUP, width), F32),
            jax.ShapeDtypeStruct((all_heads * GROUP, 1, count * rows), F32),
            jax.ShapeDtypeStruct((all_heads * GROUP, 1, count * rows), F32),
        ]
        out_specs += [away] * 3
    given = len(q_list) + len(kv_list)
    if not begin:
        aliases = {given + i: len(out_shape) + i for i in range(len(held))}
    out_shape += held
    out_specs += [near] * len(held)
    total = len(offsets) * count
    outs = pl.pallas_call(
        functools.partial(
            attend_kernel, n, count, parts, offsets, min(BLOCK, m_rows), begin, end
        ),
        out_shape=out_shape,
        in_specs=[away] * given + [near] * (0 if begin else len(held)),
        out_specs=out_specs,
        input_output_aliases=aliases,
        scratch_shapes=[
            pltpu.VMEM((total, 2, len(parts) * per, rows, width), BF16),
            pltpu.VMEM((all_heads * GROUP, 1, count * rows), F32),
            pltpu.VMEM((all_heads * GROUP, 1, count * rows), F32),
            pltpu.SMEM((count, total + 1 + SPAN // rows), jnp.int32),
            pltpu.SemaphoreType.DMA((count,)),
            pltpu.SemaphoreType.DMA((len(offsets),)),
            pltpu.SemaphoreType.DMA((len(parts), count)),
        ],
        compiler_params=pltpu.CompilerParams(vmem_limit_bytes=VMEM_LIMIT),
        cost_estimate=pl.CostEstimate(
            flops=COST * len(offsets) * len(parts), bytes_accessed=2**20, transcendentals=0
        ),
    )(*q_list, *kv_list, *(state or []))
    return tuple(outs[:3]) if end else outs


def along(block, axis, target):
    size = lax.axis_size(axis)
    return lax.ppermute(block, axis, [(i, target(i) % size) for i in range(size)])


def climb(block, d, layer):
    n, count = lax.axis_size("ctx"), lax.axis_size("head")
    edges = []
    for p in range(n):
        for h in range(count):
            edges.append((p * count + h, (p + layer) % n * count + (h + d) % count))
    return lax.ppermute(block, ("ctx", "head"), edges)


def local(queries, keys, values):
    n = lax.axis_size("ctx")
    count = lax.axis_size("head")
    me = lax.axis_index("ctx")
    swap = lambda x, d: along(x, "head", lambda i: i + d)

    kv = pack_kv(keys, values, count)
    own = [kv[0]] + [swap(kv[d], d) for d in range(1, count)]

    layer = LAYER
    up = jnp.stack([climb(x, d, layer) for d, x in enumerate(kv)])
    split = 2 if own[0].shape[1] % 2 == 0 else 1
    q_own, *q_away = pack_q(queries, count, split)
    q = [
        [q_own] + [swap(q_away[(d - 1) * split + part], d) for d in range(1, count)]
        for part in range(split)
    ]

    both = lax.optimization_barrier(jnp.stack(own))
    side = along(both, "ctx", lambda i: i + layer // 2)
    far = along(up, "ctx", lambda i: i + layer // 2)
    odd = along(up, "ctx", lambda i: i + layer - 1 if i & 1 else i + 1)
    near = jnp.where(lax.rem(me, 2) == 0, both, up)
    near = along(near, "ctx", lambda i: i ^ 1)
    side_c = along(side, "ctx", lambda i: i ^ 1)

    bit = lambda p, even, other: even + (other - even) * (p & 1)
    offsets = [
        lambda p: 0,
        lambda p: layer,
        lambda p: layer + 2,
        lambda p: bit(p, layer + 3, layer + 1),
        lambda p: bit(p, layer + 1, layer + 3),
        lambda p: 2,
        lambda p: bit(p, 3, 1),
        lambda p: bit(p, 1, 3),
    ]
    own_at, up_at, far_at, odd_at, far_c_at, side_at, near_at, side_c_at = offsets
    first = [both, up, near, side], [own_at, up_at, near_at, side_at]
    state = [x for i in range(split) for x in attend(q[i], *first, [i], split, n, None, False)]
    state, far = lax.optimization_barrier((state, far))
    far_c = along(far, "ctx", lambda i: i ^ 1)
    parts = list(range(split))
    state = attend([], [side_c, far], [side_c_at, far_at], parts, split, n, state, False)
    return attend([], [odd, far_c], [odd_at, far_c_at], parts, split, n, state, True)


def solution(mesh):
    in_specs = (
        P("ctx", "head", None, None),
        P("ctx", "head", None, None),
        P("ctx", "head", None, None),
    )
    out_specs = (P("ctx", None, "head", None), P("head", "ctx", None), P("head", "ctx", None))
    return jax.shard_map(local, mesh=mesh, in_specs=in_specs, out_specs=out_specs, check_vma=False)
```

```python
import functools
import math

import jax
import jax.numpy as jnp
from jax import lax
from jax.experimental import pallas as pl
from jax.experimental.pallas import tpu as pltpu
from jax.sharding import PartitionSpec as P

QUERY_HEADS = 32
KEY_VALUE_HEADS = 4
WIN = 8
LAYER = 4
GROUP = QUERY_HEADS // KEY_VALUE_HEADS
BF16 = jnp.bfloat16
F32 = jnp.float32
VMEM_LIMIT = 20 * 2**20
NEG = -1e30
SPAN = 256
BLOCK = 128
COST = 10**9
PACK_LIMIT = 56 * 2**20


def slot_of(head, per, count):
    return lax.rem(head // per - lax.axis_index("head") + count, count)


def place(outs, head, per, at, x):
    for d in range(len(outs)):

        @pl.when(slot_of(head, per, len(outs)) == d)
        def _():
            outs[d][at + (head % per,)] = x


def pack_kv_kernel(k_hbm, v_hbm, *refs):
    outs, (flat, wide, sems) = refs[:-3], refs[-3:]
    rows, heads, width = k_hbm.shape[1:]
    loads = [
        pltpu.make_async_copy(ref.at[0], flat.at[i], sems.at[i])
        for i, ref in enumerate((k_hbm, v_hbm))
    ]
    for load in loads:
        load.start()
    for i in range(2):
        loads[i].wait()
        wide.at[i].reshape(rows, 8, width)[:, :heads, :] = flat[i].astype(F32)
        for head in range(heads):
            x = wide[i, pl.ds(head, rows, stride=8), :].astype(BF16)
            place(outs, head, heads // len(outs), (i,), x)


def pack_kv(keys, values, count):
    rows, heads, width = keys.shape[1:]
    shape = jax.ShapeDtypeStruct((2, heads // count, rows, width), BF16)
    return pl.pallas_call(
        pack_kv_kernel,
        out_shape=(shape,) * count,
        in_specs=[pl.BlockSpec(memory_space=pl.ANY)] * 2,
        out_specs=[pl.BlockSpec(memory_space=pltpu.VMEM)] * count,
        scratch_shapes=[
            pltpu.VMEM((2, rows, heads, width), BF16),
            pltpu.VMEM((2, rows * 8, width), F32),
            pltpu.SemaphoreType.DMA((2,)),
        ],
        compiler_params=pltpu.CompilerParams(vmem_limit_bytes=PACK_LIMIT),
    )(keys, values)


def pack_q_kernel(count, q_ref, own, *away):
    rows, heads, width = q_ref.shape[1:]
    per = heads // GROUP // count
    split = len(away) // max(count - 1, 1)
    for head in range(heads // GROUP):
        x = q_ref[0, :, head * GROUP : (head + 1) * GROUP, :].astype(F32)
        x = x.reshape(rows * GROUP, width).astype(BF16)
        part, g = divmod(head % per, per // split) if away else (0, 0)
        for d in range(count):

            @pl.when(slot_of(head, per, count) == d)
            def _():
                if d:
                    away[(d - 1) * split + part][g] = x
                else:
                    own[head % per] = x


def pack_q(queries, count, split):
    rows, heads, width = queries.shape[1:]
    per = heads // GROUP // count
    own = jax.ShapeDtypeStruct((per, rows * GROUP, width), BF16)
    away = jax.ShapeDtypeStruct((per // split, rows * GROUP, width), BF16)
    outs = (own,) + (away,) * (split * (count - 1))
    return pl.pallas_call(
        functools.partial(pack_q_kernel, count),
        out_shape=outs,
        in_specs=[pl.BlockSpec(memory_space=pltpu.VMEM)],
        out_specs=[pl.BlockSpec(memory_space=pltpu.VMEM)] * len(outs),
        compiler_params=pltpu.CompilerParams(vmem_limit_bytes=VMEM_LIMIT),
    )(queries)


def start_of(pair, chunk, n, count, rows, pick):
    half = count * rows // 2
    r = chunk * rows
    return pick(r < half, 2 * pair * half + r, (2 * n - 2 - 2 * pair) * half + r)


def step_range(n, count, rows, offsets, begin, small):
    pick = lambda c, x, y: x if c else y
    found = []
    for p in range(n):
        steps = 0
        for chunk in range(count):
            mine = start_of(p, chunk, n, count, rows, pick)
            seen = sum(
                start_of((p - offset(p)) % n, c, n, count, rows, pick) < mine
                for offset in offsets
                for c in range(count)
            )
            seen = max(seen + 1 - small, 0) if begin else seen
            steps += -(-seen // small)
        found.append(steps)
    return min(found), max(found)


def attend_kernel(n, count, parts, offsets, block, begin, end, *refs):
    total = len(offsets) * count
    if begin:
        q_hbm, refs = refs[:count], refs[count:]
    kv_hbm, refs = refs[: len(offsets)], refs[len(offsets) :]
    held = 4 * len(parts)
    if not begin:
        refs = refs[held:]
    if end:
        out_hbm, max_hbm, sum_hbm = refs[:3]
        refs = refs[3:]
    states = [refs[i : i + 4] for i in range(0, held, 4)]
    if end:
        kvbuf, tops_buf, sums_buf = kv_hbm[0], *refs[held : held + 2]
        held += 2
    else:
        kvbuf = refs[held]
        held += 1
    order, qsem, ksem, osem = refs[held:]
    per, m_rows, width = states[0][0].shape[1:]
    rows = m_rows // GROUP
    small = SPAN // rows
    p = lax.axis_index("ctx")
    h = lax.axis_index("head")
    factor = math.log2(math.e) / math.sqrt(width)

    loads = []
    if begin:
        mine = q_hbm[0].at[pl.ds(parts[0] * per, per)]
        for s, ref in enumerate([mine, *q_hbm[1:]]):
            loads.append(pltpu.make_async_copy(ref, states[0][0].at[s], qsem.at[s]))
    for i, ref in enumerate([] if end else kv_hbm):
        to = kvbuf.at[pl.ds(i * count, count)]
        ref = ref.at[:, :, pl.ds(parts[0] * per, len(parts) * per)]
        loads.append(pltpu.make_async_copy(ref, to, ksem.at[i]))
    for load in loads:
        load.start()

    chunk_of = [lax.rem(h - d + count, count) for d in range(count)]
    starts = []
    for offset in offsets:
        pair = lax.rem(p - offset(p) + n, n)
        starts += [start_of(pair, chunk, n, count, rows, jnp.where) for chunk in chunk_of]
    seen, ends = [], [jnp.int32(0)]
    base = small if begin else 0
    for s in range(count):
        mine = start_of(p, chunk_of[s], n, count, rows, jnp.where)
        found = jnp.int32(0)
        if begin:
            order[s, 0] = s
            found = jnp.int32(1)
        for c in range(total):
            if not begin or c != s:
                order[s, found] = c
                found = found + (starts[c] < mine).astype(jnp.int32)
        again = order[s, jnp.maximum(found - 1, 0)]
        for t in range(small):
            order[s, found + t] = again
        seen.append(found)
        ends.append(ends[-1] + (jnp.maximum(found - base, 0) + small - 1) // small)

    def chunks_at(kind, s, g, at):
        return [kvbuf[order[s, at + t], kind, g] for t in range(small)]

    def one(part, s, g, b, k, v, left, diagonal):
        qbuf, acc, mbuf, lbuf = states[part]
        where = slice(b * block, (b + 1) * block)
        row = b * (block // GROUP)
        acc_at = s, slice(row, row + block // GROUP), slice(g * GROUP, (g + 1) * GROUP)
        score = lax.dot_general(
            qbuf[s, g, where, :], k, (((1,), (1,)), ((), ())), preferred_element_type=F32
        )
        parts = [score[:, t : t + 128] for t in range(0, small * rows, 128)]
        if diagonal:
            shape = (block // GROUP, GROUP, 128)
            col = lax.broadcasted_iota(jnp.int32, shape, 2)
            row = lax.broadcasted_iota(jnp.int32, shape, 0) + row
            for t, x in enumerate(parts):
                x = x.reshape(shape)
                if t * 128 >= rows and rows % 128 == 0:
                    x = jnp.where(t * 128 < left, x, NEG)
                else:
                    ok = col + t * 128 < left
                    if t * 128 < rows:
                        ok &= (col + t * 128 <= row) | (col + t * 128 >= rows)
                    x = jnp.where(ok, x, NEG)
                parts[t] = x.reshape(block, 128)
        top = jnp.max(functools.reduce(jnp.maximum, parts), axis=1, keepdims=True)
        if not diagonal:
            old = mbuf[s, g, where, :]
            top = jnp.maximum(old, top)
        prob = jnp.concatenate(
            [jnp.exp2((x - top) * factor).astype(BF16) for x in parts], axis=1
        )
        got = jnp.dot(prob, v, preferred_element_type=F32)
        gain, mass = got[:, :width], got[:, width:]
        if not diagonal:
            shrink = jnp.exp2((old - top) * factor)
            gain = acc[acc_at].reshape(block, width) * shrink + gain
            mass = lbuf[s, g, where, :] * shrink + mass
        mbuf[s, g, where, :] = jnp.broadcast_to(top, (block, 128))
        lbuf[s, g, where, :] = mass
        acc[acc_at] = gain.reshape(block // GROUP, GROUP, width)

    def run(s, at, found, diagonal):
        left = (found - at) * rows
        for g in range(len(parts) * per):
            k = jnp.concatenate(chunks_at(0, s, g, at), axis=0)
            v = [jnp.concatenate([x, jnp.ones_like(x)], axis=1) for x in chunks_at(1, s, g, at)]
            if not diagonal:
                v[1:] = [
                    jnp.where(t * rows < left, x, jnp.zeros_like(x))
                    for t, x in enumerate(v[1:], 1)
                ]
            v = jnp.concatenate(v, axis=0)
            for b in range(m_rows // block):
                one(g // per, s, g % per, b, k, v, left, diagonal)

    def step(t):
        s, at, found = jnp.int32(0), base + t * small, seen[0]
        for c in range(1, count):
            after = t >= ends[c]
            s = jnp.where(after, c, s)
            at = jnp.where(after, base + (t - ends[c]) * small, at)
            found = jnp.where(after, seen[c], found)
        run(s, at, found, False)

    for load in loads:
        load.wait()
    if begin:
        for s in range(count):
            run(s, 0, seen[s], True)
    if not end:
        least, most = step_range(n, count, rows, offsets, begin, small)
        for t in range(least):
            step(t)
        for t in range(least, most):

            @pl.when(t < ends[-1])
            def _():
                step(t)

        return

    saves = []
    heads = per * GROUP
    for s in range(count):
        for at in range(0, total, small):

            @pl.when(at < seen[s])
            def _():
                run(s, at, seen[s], False)

        row0 = pl.multiple_of(chunk_of[s] * rows, rows)
        for i, part in enumerate(parts):
            to = out_hbm.at[0, pl.ds(row0, rows), pl.ds(part * heads, heads)]
            saves.append(pltpu.make_async_copy(states[i][1].at[s], to, osem.at[i, s]))
            saves[-1].start()

    lane = lax.broadcasted_iota(jnp.int32, (GROUP, 128), 1)
    for s in range(count):
        picked = [jnp.zeros((GROUP, 128), F32)] * (2 * len(parts) * per)
        for r in range(rows):
            at = slice(r * GROUP, (r + 1) * GROUP)
            found = [states[i][j][s, g, at, :] for i in range(len(parts)) for g in range(per) for j in (2, 3)]
            picked = [jnp.where(lane == r, x, old) for x, old in zip(found, picked)]
        tops = jnp.concatenate(picked[0::2], axis=0)[:, :rows] * (1.0 / math.sqrt(width))
        sums = jnp.concatenate(picked[1::2], axis=0)[:, :rows]
        for d in range(count):

            @pl.when(chunk_of[s] == d)
            def _():
                tops_buf[:, 0, d * rows : (d + 1) * rows] = tops
                sums_buf[:, 0, d * rows : (d + 1) * rows] = sums
    saves.append(pltpu.make_async_copy(tops_buf, max_hbm, qsem.at[0]))
    saves.append(pltpu.make_async_copy(sums_buf, sum_hbm, ksem.at[0]))
    for save in saves[-2:]:
        save.start()
    for save in saves:
        save.wait()


def attend(q_list, kv_list, offsets, parts, split, n, state, end):
    begin = state is None
    count, all_heads, rows, width = kv_list[0].shape[0], *kv_list[0].shape[2:]
    per = all_heads // split
    m_rows = rows * GROUP
    near, away = pl.BlockSpec(memory_space=pltpu.VMEM), pl.BlockSpec(memory_space=pl.ANY)
    held = [
        jax.ShapeDtypeStruct((count, per, m_rows, width), BF16),
        jax.ShapeDtypeStruct((count, rows, per * GROUP, width), F32),
        jax.ShapeDtypeStruct((count, per, m_rows, 128), F32),
        jax.ShapeDtypeStruct((count, per, m_rows, 128), F32),
    ] * len(parts)
    out_shape, out_specs, aliases = [], [], {}
    if end:
        out_shape += [
            jax.ShapeDtypeStruct((1, count * rows, all_heads * GROUP, width), F32),
            jax.ShapeDtypeStruct((all_heads * GROUP, 1, count * rows), F32),
            jax.ShapeDtypeStruct((all_heads * GROUP, 1, count * rows), F32),
        ]
        out_specs += [away] * 3
    given = len(q_list) + len(kv_list)
    if not begin:
        aliases = {given + i: len(out_shape) + i for i in range(len(held))}
    out_shape += held
    out_specs += [near] * len(held)
    total = len(offsets) * count
    outs = pl.pallas_call(
        functools.partial(
            attend_kernel, n, count, parts, offsets, min(BLOCK, m_rows), begin, end
        ),
        out_shape=out_shape,
        in_specs=[near if end else away] * given + [near] * (0 if begin else len(held)),
        out_specs=out_specs,
        input_output_aliases=aliases,
        scratch_shapes=(
            [pltpu.VMEM((all_heads * GROUP, 1, count * rows), F32)] * 2
            if end
            else [pltpu.VMEM((total, 2, len(parts) * per, rows, width), BF16)]
        )
        + [
            pltpu.SMEM((count, total + 1 + SPAN // rows), jnp.int32),
            pltpu.SemaphoreType.DMA((count,)),
            pltpu.SemaphoreType.DMA((len(offsets),)),
            pltpu.SemaphoreType.DMA((len(parts), count)),
        ],
        compiler_params=pltpu.CompilerParams(vmem_limit_bytes=VMEM_LIMIT),
        cost_estimate=pl.CostEstimate(
            flops=COST * len(offsets) * len(parts), bytes_accessed=2**20, transcendentals=0
        ),
    )(*q_list, *kv_list, *(state or []))
    return tuple(outs[:3]) if end else outs


def along(block, axis, target):
    size = lax.axis_size(axis)
    return lax.ppermute(block, axis, [(i, target(i) % size) for i in range(size)])


def climb(block, d, layer):
    n, count = lax.axis_size("ctx"), lax.axis_size("head")
    edges = []
    for p in range(n):
        for h in range(count):
            edges.append((p * count + h, (p + layer) % n * count + (h + d) % count))
    return lax.ppermute(block, ("ctx", "head"), edges)


def local(queries, keys, values):
    n = lax.axis_size("ctx")
    count = lax.axis_size("head")
    me = lax.axis_index("ctx")
    swap = lambda x, d: along(x, "head", lambda i: i + d)

    kv = pack_kv(keys, values, count)
    own = [kv[0]] + [swap(kv[d], d) for d in range(1, count)]

    layer = LAYER
    up = jnp.stack([climb(x, d, layer) for d, x in enumerate(kv)])
    split = 2 if own[0].shape[1] % 2 == 0 else 1
    q_own, *q_away = pack_q(queries, count, split)
    q = [
        [q_own] + [swap(q_away[(d - 1) * split + part], d) for d in range(1, count)]
        for part in range(split)
    ]

    both = lax.optimization_barrier(jnp.stack(own))
    side = along(both, "ctx", lambda i: i + layer // 2)
    far = along(up, "ctx", lambda i: i + layer // 2)
    odd = along(up, "ctx", lambda i: i + layer - 1 if i & 1 else i + 1)
    near = jnp.where(lax.rem(me, 2) == 0, both, up)
    near = along(near, "ctx", lambda i: i ^ 1)
    side_c = along(side, "ctx", lambda i: i ^ 1)

    bit = lambda p, even, other: even + (other - even) * (p & 1)
    offsets = [
        lambda p: 0,
        lambda p: layer,
        lambda p: layer + 2,
        lambda p: bit(p, layer + 3, layer + 1),
        lambda p: bit(p, layer + 1, layer + 3),
        lambda p: 2,
        lambda p: bit(p, 3, 1),
        lambda p: bit(p, 1, 3),
    ]
    own_at, up_at, far_at, odd_at, far_c_at, side_at, near_at, side_c_at = offsets
    blocks = dict(
        own=(both, own_at), up=(up, up_at), near=(near, near_at), side=(side, side_at),
        side_c=(side_c, side_c_at), odd=(odd, odd_at),
    )

    def take(names):
        return [blocks[x][0] for x in names], [blocks[x][1] for x in names]

    soon, late = ["own", "up", "near", "side"], ["side_c"]
    state = []
    for i in range(split):
        last = i == split - 1
        part = attend(q[i], *take(soon + late if last else soon), [i], split, n, None, False)
        if not last:
            part = attend([], *take(late), [i], split, n, part, False)
            part, q[i + 1] = lax.optimization_barrier((part, q[i + 1]))
        state += part
    state, far = lax.optimization_barrier((state, far))
    far_c = along(far, "ctx", lambda i: i ^ 1)
    parts = list(range(split))
    state = attend([], [odd, far], [odd_at, far_at], parts, split, n, state, False)
    return attend([], [far_c], [far_c_at], parts, split, n, state, True)


def solution(mesh):
    in_specs = (
        P("ctx", "head", None, None),
        P("ctx", "head", None, None),
        P("ctx", "head", None, None),
    )
    out_specs = (P("ctx", None, "head", None), P("head", "ctx", None), P("head", "ctx", None))
    return jax.shard_map(local, mesh=mesh, in_specs=in_specs, out_specs=out_specs, check_vma=False)
```

```python
import functools
import math

import jax
import jax.numpy as jnp
from jax import lax
from jax.experimental import pallas as pl
from jax.experimental.pallas import tpu as pltpu
from jax.sharding import PartitionSpec as P

QUERY_HEADS = 32
KEY_VALUE_HEADS = 4
WIN = 8
LAYER = 4
GROUP = QUERY_HEADS // KEY_VALUE_HEADS
BF16 = jnp.bfloat16
F32 = jnp.float32
VMEM_LIMIT = 20 * 2**20
NEG = -1e30
SPAN = 256
BLOCK = 128
COST = 10**9


def slot_of(head, per, count):
    return lax.rem(head // per - lax.axis_index("head") + count, count)


def pack_q_kernel(count, q_ref, own, *away):
    rows, heads, width = q_ref.shape[1:]
    per = heads // GROUP // count
    split = len(away) // max(count - 1, 1)
    for head in range(heads // GROUP):
        x = q_ref[0, :, head * GROUP : (head + 1) * GROUP, :].astype(F32)
        x = x.reshape(rows * GROUP, width).astype(BF16)
        part, g = divmod(head % per, per // split) if away else (0, 0)
        for d in range(count):

            @pl.when(slot_of(head, per, count) == d)
            def _():
                if d:
                    away[(d - 1) * split + part][g] = x
                else:
                    own[head % per] = x


def pack_q(queries, count, split):
    rows, heads, width = queries.shape[1:]
    per = heads // GROUP // count
    own = jax.ShapeDtypeStruct((per, rows * GROUP, width), BF16)
    away = jax.ShapeDtypeStruct((per // split, rows * GROUP, width), BF16)
    outs = (own,) + (away,) * (split * (count - 1))
    return pl.pallas_call(
        functools.partial(pack_q_kernel, count),
        out_shape=outs,
        in_specs=[pl.BlockSpec(memory_space=pltpu.VMEM)],
        out_specs=[pl.BlockSpec(memory_space=pltpu.VMEM)] * len(outs),
        compiler_params=pltpu.CompilerParams(vmem_limit_bytes=VMEM_LIMIT),
    )(queries)


def start_of(pair, chunk, n, count, rows, pick):
    half = count * rows // 2
    r = chunk * rows
    return pick(r < half, 2 * pair * half + r, (2 * n - 2 - 2 * pair) * half + r)


def step_range(n, count, rows, offsets, begin, small):
    pick = lambda c, x, y: x if c else y
    found = []
    for p in range(n):
        steps = 0
        for chunk in range(count):
            mine = start_of(p, chunk, n, count, rows, pick)
            seen = sum(
                start_of((p - offset(p)) % n, c, n, count, rows, pick) < mine
                for offset in offsets
                for c in range(count)
            )
            seen = max(seen + 1 - small, 0) if begin else seen
            steps += -(-seen // small)
        found.append(steps)
    return min(found), max(found)


def attend_kernel(n, count, parts, offsets, block, begin, end, *refs):
    total = len(offsets) * count
    if begin:
        q_hbm, refs = refs[:count], refs[count:]
    kv_hbm, refs = refs[: len(offsets)], refs[len(offsets) :]
    held = 4 * len(parts)
    if not begin:
        refs = refs[held:]
    if end:
        out_hbm, max_hbm, sum_hbm = refs[:3]
        refs = refs[3:]
    states = [refs[i : i + 4] for i in range(0, held, 4)]
    if end:
        kvbuf, tops_buf, sums_buf = kv_hbm[0], *refs[held : held + 2]
        held += 2
    else:
        kvbuf = refs[held]
        held += 1
    order, qsem, ksem, osem = refs[held:]
    per, m_rows, width = states[0][0].shape[1:]
    rows = m_rows // GROUP
    small = SPAN // rows
    p = lax.axis_index("ctx")
    h = lax.axis_index("head")
    factor = math.log2(math.e) / math.sqrt(width)

    loads = []
    if begin:
        mine = q_hbm[0].at[pl.ds(parts[0] * per, per)]
        for s, ref in enumerate([mine, *q_hbm[1:]]):
            loads.append(pltpu.make_async_copy(ref, states[0][0].at[s], qsem.at[s]))
    for i, ref in enumerate([] if end else kv_hbm):
        to = kvbuf.at[pl.ds(i * count, count)]
        ref = ref.at[:, :, pl.ds(parts[0] * per, len(parts) * per)]
        loads.append(pltpu.make_async_copy(ref, to, ksem.at[i]))
    for load in loads:
        load.start()

    chunk_of = [lax.rem(h - d + count, count) for d in range(count)]
    starts = []
    for offset in offsets:
        pair = lax.rem(p - offset(p) + n, n)
        starts += [start_of(pair, chunk, n, count, rows, jnp.where) for chunk in chunk_of]
    seen, ends = [], [jnp.int32(0)]
    base = small if begin else 0
    for s in range(count):
        mine = start_of(p, chunk_of[s], n, count, rows, jnp.where)
        found = jnp.int32(0)
        if begin:
            order[s, 0] = s
            found = jnp.int32(1)
        for c in range(total):
            if not begin or c != s:
                order[s, found] = c
                found = found + (starts[c] < mine).astype(jnp.int32)
        again = order[s, jnp.maximum(found - 1, 0)]
        for t in range(small):
            order[s, found + t] = again
        seen.append(found)
        ends.append(ends[-1] + (jnp.maximum(found - base, 0) + small - 1) // small)

    def chunks_at(kind, s, g, at):
        return [kvbuf[order[s, at + t], kind, g] for t in range(small)]

    def one(part, s, g, b, k, v, left, diagonal):
        qbuf, acc, mbuf, lbuf = states[part]
        where = slice(b * block, (b + 1) * block)
        row = b * (block // GROUP)
        acc_at = s, slice(row, row + block // GROUP), slice(g * GROUP, (g + 1) * GROUP)
        score = lax.dot_general(
            qbuf[s, g, where, :], k, (((1,), (1,)), ((), ())), preferred_element_type=F32
        )
        parts = [score[:, t : t + 128] for t in range(0, small * rows, 128)]
        if diagonal:
            shape = (block // GROUP, GROUP, 128)
            col = lax.broadcasted_iota(jnp.int32, shape, 2)
            row = lax.broadcasted_iota(jnp.int32, shape, 0) + row
            for t, x in enumerate(parts):
                x = x.reshape(shape)
                if t * 128 >= rows and rows % 128 == 0:
                    x = jnp.where(t * 128 < left, x, NEG)
                else:
                    ok = col + t * 128 < left
                    if t * 128 < rows:
                        ok &= (col + t * 128 <= row) | (col + t * 128 >= rows)
                    x = jnp.where(ok, x, NEG)
                parts[t] = x.reshape(block, 128)
        top = jnp.max(functools.reduce(jnp.maximum, parts), axis=1, keepdims=True)
        if not diagonal:
            old = mbuf[s, g, where, :]
            top = jnp.maximum(old, top)
        prob = jnp.concatenate(
            [jnp.exp2((x - top) * factor).astype(BF16) for x in parts], axis=1
        )
        got = jnp.dot(prob, v, preferred_element_type=F32)
        gain, mass = got[:, :width], got[:, width:]
        if not diagonal:
            shrink = jnp.exp2((old - top) * factor)
            gain = acc[acc_at].reshape(block, width) * shrink + gain
            mass = lbuf[s, g, where, :] * shrink + mass
        mbuf[s, g, where, :] = jnp.broadcast_to(top, (block, 128))
        lbuf[s, g, where, :] = mass
        acc[acc_at] = gain.reshape(block // GROUP, GROUP, width)

    def run(s, at, found, diagonal):
        left = (found - at) * rows
        for g in range(len(parts) * per):
            k = jnp.concatenate(chunks_at(0, s, g, at), axis=0)
            v = [jnp.concatenate([x, jnp.ones_like(x)], axis=1) for x in chunks_at(1, s, g, at)]
            if not diagonal:
                v[1:] = [
                    jnp.where(t * rows < left, x, jnp.zeros_like(x))
                    for t, x in enumerate(v[1:], 1)
                ]
            v = jnp.concatenate(v, axis=0)
            for b in range(m_rows // block):
                one(g // per, s, g % per, b, k, v, left, diagonal)

    def step(t):
        s, at, found = jnp.int32(0), base + t * small, seen[0]
        for c in range(1, count):
            after = t >= ends[c]
            s = jnp.where(after, c, s)
            at = jnp.where(after, base + (t - ends[c]) * small, at)
            found = jnp.where(after, seen[c], found)
        run(s, at, found, False)

    for load in loads:
        load.wait()
    if begin:
        for s in range(count):
            run(s, 0, seen[s], True)
    if not end:
        least, most = step_range(n, count, rows, offsets, begin, small)
        for t in range(least):
            step(t)
        for t in range(least, most):

            @pl.when(t < ends[-1])
            def _():
                step(t)

        return

    saves = []
    heads = per * GROUP
    for s in range(count):
        for at in range(0, total, small):

            @pl.when(at < seen[s])
            def _():
                run(s, at, seen[s], False)

        row0 = pl.multiple_of(chunk_of[s] * rows, rows)
        for i, part in enumerate(parts):
            to = out_hbm.at[0, pl.ds(row0, rows), pl.ds(part * heads, heads)]
            saves.append(pltpu.make_async_copy(states[i][1].at[s], to, osem.at[i, s]))
            saves[-1].start()

    lane = lax.broadcasted_iota(jnp.int32, (GROUP, 128), 1)
    for s in range(count):
        picked = [jnp.zeros((GROUP, 128), F32)] * (2 * len(parts) * per)
        for r in range(rows):
            at = slice(r * GROUP, (r + 1) * GROUP)
            found = [states[i][j][s, g, at, :] for i in range(len(parts)) for g in range(per) for j in (2, 3)]
            picked = [jnp.where(lane == r, x, old) for x, old in zip(found, picked)]
        tops = jnp.concatenate(picked[0::2], axis=0)[:, :rows] * (1.0 / math.sqrt(width))
        sums = jnp.concatenate(picked[1::2], axis=0)[:, :rows]
        for d in range(count):

            @pl.when(chunk_of[s] == d)
            def _():
                tops_buf[:, 0, d * rows : (d + 1) * rows] = tops
                sums_buf[:, 0, d * rows : (d + 1) * rows] = sums
    saves.append(pltpu.make_async_copy(tops_buf, max_hbm, qsem.at[0]))
    saves.append(pltpu.make_async_copy(sums_buf, sum_hbm, ksem.at[0]))
    for save in saves[-2:]:
        save.start()
    for save in saves:
        save.wait()


def attend(q_list, kv_list, offsets, parts, split, n, state, end):
    begin = state is None
    count, all_heads, rows, width = kv_list[0].shape[0], *kv_list[0].shape[2:]
    per = all_heads // split
    m_rows = rows * GROUP
    near, away = pl.BlockSpec(memory_space=pltpu.VMEM), pl.BlockSpec(memory_space=pl.ANY)
    held = [
        jax.ShapeDtypeStruct((count, per, m_rows, width), BF16),
        jax.ShapeDtypeStruct((count, rows, per * GROUP, width), F32),
        jax.ShapeDtypeStruct((count, per, m_rows, 128), F32),
        jax.ShapeDtypeStruct((count, per, m_rows, 128), F32),
    ] * len(parts)
    out_shape, out_specs, aliases = [], [], {}
    if end:
        out_shape += [
            jax.ShapeDtypeStruct((1, count * rows, all_heads * GROUP, width), F32),
            jax.ShapeDtypeStruct((all_heads * GROUP, 1, count * rows), F32),
            jax.ShapeDtypeStruct((all_heads * GROUP, 1, count * rows), F32),
        ]
        out_specs += [away] * 3
    given = len(q_list) + len(kv_list)
    if not begin:
        aliases = {given + i: len(out_shape) + i for i in range(len(held))}
    out_shape += held
    out_specs += [near] * len(held)
    total = len(offsets) * count
    outs = pl.pallas_call(
        functools.partial(
            attend_kernel, n, count, parts, offsets, min(BLOCK, m_rows), begin, end
        ),
        out_shape=out_shape,
        in_specs=[near if end else away] * given + [near] * (0 if begin else len(held)),
        out_specs=out_specs,
        input_output_aliases=aliases,
        scratch_shapes=(
            [pltpu.VMEM((all_heads * GROUP, 1, count * rows), F32)] * 2
            if end
            else [pltpu.VMEM((total, 2, len(parts) * per, rows, width), BF16)]
        )
        + [
            pltpu.SMEM((count, total + 1 + SPAN // rows), jnp.int32),
            pltpu.SemaphoreType.DMA((count,)),
            pltpu.SemaphoreType.DMA((len(offsets),)),
            pltpu.SemaphoreType.DMA((len(parts), count)),
        ],
        compiler_params=pltpu.CompilerParams(vmem_limit_bytes=VMEM_LIMIT),
        cost_estimate=pl.CostEstimate(
            flops=COST * len(offsets) * len(parts), bytes_accessed=2**20, transcendentals=0
        ),
    )(*q_list, *kv_list, *(state or []))
    return tuple(outs[:3]) if end else outs


def along(block, axis, target):
    size = lax.axis_size(axis)
    return lax.ppermute(block, axis, [(i, target(i) % size) for i in range(size)])


def climb(block, d, layer):
    n, count = lax.axis_size("ctx"), lax.axis_size("head")
    edges = []
    for p in range(n):
        for h in range(count):
            edges.append((p * count + h, (p + layer) % n * count + (h + d) % count))
    return lax.ppermute(block, ("ctx", "head"), edges)


def local(queries, keys, values):
    n = lax.axis_size("ctx")
    count = lax.axis_size("head")
    me = lax.axis_index("ctx")
    swap = lambda x, d: along(x, "head", lambda i: i + d)

    mine = lax.axis_index("head")

    def heads_of(x, d):
        size = x.shape[2] // count
        return lax.dynamic_slice_in_dim(x[0], lax.rem(mine + d, count) * size, size, axis=1)

    kv = [
        jnp.stack([heads_of(keys, d), heads_of(values, d)]).transpose(0, 2, 1, 3)
        for d in range(count)
    ]
    own = [kv[0]] + [swap(kv[d], d) for d in range(1, count)]

    layer = LAYER
    up = jnp.stack([climb(x, d, layer) for d, x in enumerate(kv)])
    split = 2 if own[0].shape[1] % 2 == 0 else 1
    q_own, *q_away = pack_q(queries, count, split)
    q = [
        [q_own] + [swap(q_away[(d - 1) * split + part], d) for d in range(1, count)]
        for part in range(split)
    ]

    both = lax.optimization_barrier(jnp.stack(own))
    side = along(both, "ctx", lambda i: i + layer // 2)
    far = along(up, "ctx", lambda i: i + layer // 2)
    odd = along(up, "ctx", lambda i: i + layer - 1 if i & 1 else i + 1)
    near = jnp.where(lax.rem(me, 2) == 0, both, up)
    near = along(near, "ctx", lambda i: i ^ 1)
    side_c = along(side, "ctx", lambda i: i ^ 1)

    bit = lambda p, even, other: even + (other - even) * (p & 1)
    offsets = [
        lambda p: 0,
        lambda p: layer,
        lambda p: layer + 2,
        lambda p: bit(p, layer + 3, layer + 1),
        lambda p: bit(p, layer + 1, layer + 3),
        lambda p: 2,
        lambda p: bit(p, 3, 1),
        lambda p: bit(p, 1, 3),
    ]
    own_at, up_at, far_at, odd_at, far_c_at, side_at, near_at, side_c_at = offsets
    blocks = dict(
        own=(both, own_at), up=(up, up_at), near=(near, near_at), side=(side, side_at),
        side_c=(side_c, side_c_at), odd=(odd, odd_at),
    )

    def take(names):
        return [blocks[x][0] for x in names], [blocks[x][1] for x in names]

    soon, late = ["own", "up", "near", "side"], ["side_c"]
    state = []
    for i in range(split):
        last = i == split - 1
        part = attend(q[i], *take(soon + late if last else soon), [i], split, n, None, False)
        if not last:
            part = attend([], *take(late), [i], split, n, part, False)
            part, q[i + 1] = lax.optimization_barrier((part, q[i + 1]))
        state += part
    state, far = lax.optimization_barrier((state, far))
    far_c = along(far, "ctx", lambda i: i ^ 1)
    parts = list(range(split))
    state = attend([], [odd, far], [odd_at, far_at], parts, split, n, state, False)
    return attend([], [far_c], [far_c_at], parts, split, n, state, True)


def solution(mesh):
    in_specs = (
        P("ctx", "head", None, None),
        P("ctx", "head", None, None),
        P("ctx", "head", None, None),
    )
    out_specs = (P("ctx", None, "head", None), P("head", "ctx", None), P("head", "ctx", None))
    return jax.shard_map(local, mesh=mesh, in_specs=in_specs, out_specs=out_specs, check_vma=False)
```

```python
import functools
import math

import jax
import jax.numpy as jnp
from jax import lax
from jax.experimental import pallas as pl
from jax.experimental.pallas import tpu as pltpu
from jax.sharding import PartitionSpec as P

QUERY_HEADS = 32
KEY_VALUE_HEADS = 4
WIN = 8
LAYER = 4
GROUP = QUERY_HEADS // KEY_VALUE_HEADS
BF16 = jnp.bfloat16
F32 = jnp.float32
VMEM_LIMIT = 20 * 2**20
NEG = -1e30
SPAN = 256
BLOCK = 256
COST = 10**9


def slot_of(head, per, count):
    return lax.rem(head // per - lax.axis_index("head") + count, count)


def pack_q_kernel(count, q_ref, own, *away):
    rows, heads, width = q_ref.shape[1:]
    per = heads // GROUP // count
    split = len(away) // max(count - 1, 1)
    for head in range(heads // GROUP):
        x = q_ref[0, :, head * GROUP : (head + 1) * GROUP, :].astype(F32)
        x = x.reshape(rows * GROUP, width).astype(BF16)
        part, g = divmod(head % per, per // split) if away else (0, 0)
        for d in range(count):

            @pl.when(slot_of(head, per, count) == d)
            def _():
                if d:
                    away[(d - 1) * split + part][g] = x
                else:
                    own[head % per] = x


def pack_q(queries, count, split):
    rows, heads, width = queries.shape[1:]
    per = heads // GROUP // count
    own = jax.ShapeDtypeStruct((per, rows * GROUP, width), BF16)
    away = jax.ShapeDtypeStruct((per // split, rows * GROUP, width), BF16)
    outs = (own,) + (away,) * (split * (count - 1))
    return pl.pallas_call(
        functools.partial(pack_q_kernel, count),
        out_shape=outs,
        in_specs=[pl.BlockSpec(memory_space=pltpu.VMEM)],
        out_specs=[pl.BlockSpec(memory_space=pltpu.VMEM)] * len(outs),
        compiler_params=pltpu.CompilerParams(vmem_limit_bytes=VMEM_LIMIT),
    )(queries)


def start_of(pair, chunk, n, count, rows, pick):
    half = count * rows // 2
    r = chunk * rows
    return pick(r < half, 2 * pair * half + r, (2 * n - 2 - 2 * pair) * half + r)


def step_range(n, count, rows, offsets, begin, small):
    pick = lambda c, x, y: x if c else y
    found = []
    for p in range(n):
        steps = 0
        for chunk in range(count):
            mine = start_of(p, chunk, n, count, rows, pick)
            seen = sum(
                start_of((p - offset(p)) % n, c, n, count, rows, pick) < mine
                for offset in offsets
                for c in range(count)
            )
            seen = max(seen + 1 - small, 0) if begin else seen
            steps += -(-seen // small)
        found.append(steps)
    return min(found), max(found)


def attend_kernel(n, count, parts, offsets, block, begin, end, *refs):
    total = len(offsets) * count
    if begin:
        q_hbm, refs = refs[:count], refs[count:]
    kv_hbm, refs = refs[: len(offsets)], refs[len(offsets) :]
    held = 4 * len(parts)
    if not begin:
        refs = refs[held:]
    if end:
        out_hbm, max_hbm, sum_hbm = refs[:3]
        refs = refs[3:]
    states = [refs[i : i + 4] for i in range(0, held, 4)]
    if end:
        kvbuf, tops_buf, sums_buf = kv_hbm[0], *refs[held : held + 2]
        held += 2
    else:
        kvbuf = refs[held]
        held += 1
    order, qsem, ksem, osem = refs[held:]
    per, m_rows, width = states[0][0].shape[1:]
    rows = m_rows // GROUP
    small = SPAN // rows
    p = lax.axis_index("ctx")
    h = lax.axis_index("head")
    factor = math.log2(math.e) / math.sqrt(width)

    loads = []
    if begin:
        mine = q_hbm[0].at[pl.ds(parts[0] * per, per)]
        for s, ref in enumerate([mine, *q_hbm[1:]]):
            loads.append(pltpu.make_async_copy(ref, states[0][0].at[s], qsem.at[s]))
    for i, ref in enumerate([] if end else kv_hbm):
        to = kvbuf.at[pl.ds(i * count, count)]
        ref = ref.at[:, :, pl.ds(parts[0] * per, len(parts) * per)]
        loads.append(pltpu.make_async_copy(ref, to, ksem.at[i]))
    for load in loads:
        load.start()

    chunk_of = [lax.rem(h - d + count, count) for d in range(count)]
    starts = []
    for offset in offsets:
        pair = lax.rem(p - offset(p) + n, n)
        starts += [start_of(pair, chunk, n, count, rows, jnp.where) for chunk in chunk_of]
    seen, ends = [], [jnp.int32(0)]
    base = small if begin else 0
    for s in range(count):
        mine = start_of(p, chunk_of[s], n, count, rows, jnp.where)
        found = jnp.int32(0)
        if begin:
            order[s, 0] = s
            found = jnp.int32(1)
        for c in range(total):
            if not begin or c != s:
                order[s, found] = c
                found = found + (starts[c] < mine).astype(jnp.int32)
        again = order[s, jnp.maximum(found - 1, 0)]
        for t in range(small):
            order[s, found + t] = again
        seen.append(found)
        ends.append(ends[-1] + (jnp.maximum(found - base, 0) + small - 1) // small)

    def chunks_at(kind, s, g, at):
        return [kvbuf[order[s, at + t], kind, g] for t in range(small)]

    def one(part, s, g, b, k, v, left, diagonal):
        qbuf, acc, mbuf, lbuf = states[part]
        where = slice(b * block, (b + 1) * block)
        row = b * (block // GROUP)
        acc_at = s, slice(row, row + block // GROUP), slice(g * GROUP, (g + 1) * GROUP)
        score = lax.dot_general(
            qbuf[s, g, where, :], k, (((1,), (1,)), ((), ())), preferred_element_type=F32
        )
        parts = [score[:, t : t + 128] for t in range(0, small * rows, 128)]
        if diagonal:
            shape = (block // GROUP, GROUP, 128)
            col = lax.broadcasted_iota(jnp.int32, shape, 2)
            row = lax.broadcasted_iota(jnp.int32, shape, 0) + row
            for t, x in enumerate(parts):
                x = x.reshape(shape)
                if t * 128 >= rows and rows % 128 == 0:
                    x = jnp.where(t * 128 < left, x, NEG)
                else:
                    ok = col + t * 128 < left
                    if t * 128 < rows:
                        ok &= (col + t * 128 <= row) | (col + t * 128 >= rows)
                    x = jnp.where(ok, x, NEG)
                parts[t] = x.reshape(block, 128)
        top = jnp.max(functools.reduce(jnp.maximum, parts), axis=1, keepdims=True)
        if not diagonal:
            old = mbuf[s, g, where, :]
            top = jnp.maximum(old, top)
        prob = jnp.concatenate(
            [jnp.exp2((x - top) * factor).astype(BF16) for x in parts], axis=1
        )
        got = jnp.dot(prob, v, preferred_element_type=F32)
        gain, mass = got[:, :width], got[:, width:]
        if not diagonal:
            shrink = jnp.exp2((old - top) * factor)
            gain = acc[acc_at].reshape(block, width) * shrink + gain
            mass = lbuf[s, g, where, :] * shrink + mass
        mbuf[s, g, where, :] = jnp.broadcast_to(top, (block, 128))
        lbuf[s, g, where, :] = mass
        acc[acc_at] = gain.reshape(block // GROUP, GROUP, width)

    def run(s, at, found, diagonal):
        left = (found - at) * rows
        for g in range(len(parts) * per):
            k = jnp.concatenate(chunks_at(0, s, g, at), axis=0)
            v = [jnp.concatenate([x, jnp.ones_like(x)], axis=1) for x in chunks_at(1, s, g, at)]
            if not diagonal:
                v[1:] = [
                    jnp.where(t * rows < left, x, jnp.zeros_like(x))
                    for t, x in enumerate(v[1:], 1)
                ]
            v = jnp.concatenate(v, axis=0)
            for b in range(m_rows // block):
                one(g // per, s, g % per, b, k, v, left, diagonal)

    def step(t):
        s, at, found = jnp.int32(0), base + t * small, seen[0]
        for c in range(1, count):
            after = t >= ends[c]
            s = jnp.where(after, c, s)
            at = jnp.where(after, base + (t - ends[c]) * small, at)
            found = jnp.where(after, seen[c], found)
        run(s, at, found, False)

    for load in loads:
        load.wait()
    if begin:
        for s in range(count):
            run(s, 0, seen[s], True)
    if not end:
        least, most = step_range(n, count, rows, offsets, begin, small)
        for t in range(least):
            step(t)
        for t in range(least, most):

            @pl.when(t < ends[-1])
            def _():
                step(t)

        return

    saves = []
    heads = per * GROUP
    for s in range(count):
        for at in range(0, total, small):

            @pl.when(at < seen[s])
            def _():
                run(s, at, seen[s], False)

        row0 = pl.multiple_of(chunk_of[s] * rows, rows)
        for i, part in enumerate(parts):
            to = out_hbm.at[0, pl.ds(row0, rows), pl.ds(part * heads, heads)]
            saves.append(pltpu.make_async_copy(states[i][1].at[s], to, osem.at[i, s]))
            saves[-1].start()

    lane = lax.broadcasted_iota(jnp.int32, (GROUP, 128), 1)
    for s in range(count):
        picked = [jnp.zeros((GROUP, 128), F32)] * (2 * len(parts) * per)
        for r in range(rows):
            at = slice(r * GROUP, (r + 1) * GROUP)
            found = [states[i][j][s, g, at, :] for i in range(len(parts)) for g in range(per) for j in (2, 3)]
            picked = [jnp.where(lane == r, x, old) for x, old in zip(found, picked)]
        tops = jnp.concatenate(picked[0::2], axis=0)[:, :rows] * (1.0 / math.sqrt(width))
        sums = jnp.concatenate(picked[1::2], axis=0)[:, :rows]
        for d in range(count):

            @pl.when(chunk_of[s] == d)
            def _():
                tops_buf[:, 0, d * rows : (d + 1) * rows] = tops
                sums_buf[:, 0, d * rows : (d + 1) * rows] = sums
    saves.append(pltpu.make_async_copy(tops_buf, max_hbm, qsem.at[0]))
    saves.append(pltpu.make_async_copy(sums_buf, sum_hbm, ksem.at[0]))
    for save in saves[-2:]:
        save.start()
    for save in saves:
        save.wait()


def attend(q_list, kv_list, offsets, parts, split, n, state, end):
    begin = state is None
    count, all_heads, rows, width = kv_list[0].shape[0], *kv_list[0].shape[2:]
    per = all_heads // split
    m_rows = rows * GROUP
    near, away = pl.BlockSpec(memory_space=pltpu.VMEM), pl.BlockSpec(memory_space=pl.ANY)
    held = [
        jax.ShapeDtypeStruct((count, per, m_rows, width), BF16),
        jax.ShapeDtypeStruct((count, rows, per * GROUP, width), F32),
        jax.ShapeDtypeStruct((count, per, m_rows, 128), F32),
        jax.ShapeDtypeStruct((count, per, m_rows, 128), F32),
    ] * len(parts)
    out_shape, out_specs, aliases = [], [], {}
    if end:
        out_shape += [
            jax.ShapeDtypeStruct((1, count * rows, all_heads * GROUP, width), F32),
            jax.ShapeDtypeStruct((all_heads * GROUP, 1, count * rows), F32),
            jax.ShapeDtypeStruct((all_heads * GROUP, 1, count * rows), F32),
        ]
        out_specs += [away] * 3
    given = len(q_list) + len(kv_list)
    if not begin:
        aliases = {given + i: len(out_shape) + i for i in range(len(held))}
    out_shape += held
    out_specs += [near] * len(held)
    total = len(offsets) * count
    outs = pl.pallas_call(
        functools.partial(
            attend_kernel, n, count, parts, offsets, min(BLOCK, m_rows), begin, end
        ),
        out_shape=out_shape,
        in_specs=[near if end else away] * given + [near] * (0 if begin else len(held)),
        out_specs=out_specs,
        input_output_aliases=aliases,
        scratch_shapes=(
            [pltpu.VMEM((all_heads * GROUP, 1, count * rows), F32)] * 2
            if end
            else [pltpu.VMEM((total, 2, len(parts) * per, rows, width), BF16)]
        )
        + [
            pltpu.SMEM((count, total + 1 + SPAN // rows), jnp.int32),
            pltpu.SemaphoreType.DMA((count,)),
            pltpu.SemaphoreType.DMA((len(offsets),)),
            pltpu.SemaphoreType.DMA((len(parts), count)),
        ],
        compiler_params=pltpu.CompilerParams(vmem_limit_bytes=VMEM_LIMIT),
        cost_estimate=pl.CostEstimate(
            flops=COST * len(offsets) * len(parts), bytes_accessed=2**20, transcendentals=0
        ),
    )(*q_list, *kv_list, *(state or []))
    return tuple(outs[:3]) if end else outs


def along(block, axis, target):
    size = lax.axis_size(axis)
    return lax.ppermute(block, axis, [(i, target(i) % size) for i in range(size)])


def climb(block, d, layer):
    n, count = lax.axis_size("ctx"), lax.axis_size("head")
    edges = []
    for p in range(n):
        for h in range(count):
            edges.append((p * count + h, (p + layer) % n * count + (h + d) % count))
    return lax.ppermute(block, ("ctx", "head"), edges)


def local(queries, keys, values):
    n = lax.axis_size("ctx")
    count = lax.axis_size("head")
    me = lax.axis_index("ctx")
    swap = lambda x, d: along(x, "head", lambda i: i + d)

    mine = lax.axis_index("head")

    def heads_of(x, d):
        size = x.shape[2] // count
        return lax.dynamic_slice_in_dim(x[0], lax.rem(mine + d, count) * size, size, axis=1)

    kv = [
        jnp.stack([heads_of(keys, d), heads_of(values, d)]).transpose(0, 2, 1, 3)
        for d in range(count)
    ]
    own = [kv[0]] + [swap(kv[d], d) for d in range(1, count)]

    layer = LAYER
    up = jnp.stack([climb(x, d, layer) for d, x in enumerate(kv)])
    split = 2 if own[0].shape[1] % 2 == 0 else 1
    q_own, *q_away = pack_q(queries, count, split)
    q = [
        [q_own] + [swap(q_away[(d - 1) * split + part], d) for d in range(1, count)]
        for part in range(split)
    ]

    both = lax.optimization_barrier(jnp.stack(own))
    side = along(both, "ctx", lambda i: i + layer // 2)
    far = along(up, "ctx", lambda i: i + layer // 2)
    odd = along(up, "ctx", lambda i: i + layer - 1 if i & 1 else i + 1)
    near = jnp.where(lax.rem(me, 2) == 0, both, up)
    near = along(near, "ctx", lambda i: i ^ 1)
    side_c = along(side, "ctx", lambda i: i ^ 1)

    bit = lambda p, even, other: even + (other - even) * (p & 1)
    offsets = [
        lambda p: 0,
        lambda p: layer,
        lambda p: layer + 2,
        lambda p: bit(p, layer + 3, layer + 1),
        lambda p: bit(p, layer + 1, layer + 3),
        lambda p: 2,
        lambda p: bit(p, 3, 1),
        lambda p: bit(p, 1, 3),
    ]
    own_at, up_at, far_at, odd_at, far_c_at, side_at, near_at, side_c_at = offsets
    blocks = dict(
        own=(both, own_at), up=(up, up_at), near=(near, near_at), side=(side, side_at),
        side_c=(side_c, side_c_at), odd=(odd, odd_at),
    )

    def take(names):
        return [blocks[x][0] for x in names], [blocks[x][1] for x in names]

    soon, late = ["own", "up", "near"], ["side", "side_c"]
    state = []
    for i in range(split):
        last = i == split - 1
        part = attend(q[i], *take(soon + late if last else soon), [i], split, n, None, False)
        if not last:
            part = attend([], *take(late), [i], split, n, part, False)
            part, q[i + 1] = lax.optimization_barrier((part, q[i + 1]))
        state += part
    state, far = lax.optimization_barrier((state, far))
    far_c = along(far, "ctx", lambda i: i ^ 1)
    parts = list(range(split))
    state = attend([], [odd, far], [odd_at, far_at], parts, split, n, state, False)
    return attend([], [far_c], [far_c_at], parts, split, n, state, True)


def solution(mesh):
    in_specs = (
        P("ctx", "head", None, None),
        P("ctx", "head", None, None),
        P("ctx", "head", None, None),
    )
    out_specs = (P("ctx", None, "head", None), P("head", "ctx", None), P("head", "ctx", None))
    return jax.shard_map(local, mesh=mesh, in_specs=in_specs, out_specs=out_specs, check_vma=False)
```
